512 devices in a mesh: crop: 16 (over x, y_lo, core), dap: 32 (over y_hi, z).
Axes of the slice: x: 4, y: 4 (y_hi: 2, y_lo: 2; y = y_hi * 2 + y_lo), z: 16, core: 2. Of those that a mesh axis runs over, the one named last changes fastest.
Arguments:
- pair: float32 [16, 128, 128, 128], P('crop', 'dap'), may hold values from -6 to 6
- pair_grad: float32 [16, 128, 128, 128], P('crop', 'dap'), may hold values from -6 to 6
- norm_gain: float32 [2, 128], replicated, may hold values from 0.5 to 1.5
- norm_shift: float32 [2, 128], replicated, may hold values from -3 to 3
- proj_weight: float32 [2, 4, 128, 128], replicated, may hold values from -0.5 to 0.5
- bias_weight: float32 [2, 4, 128], replicated, may hold values from -0.5 to 0.5
- gate_shift: float32 [2, 128], replicated, may hold values from -4 to 4
- out_weight: float32 [2, 128, 128], replicated, may hold values from -0.5 to 0.5
- out_shift: float32 [2, 128], replicated, may hold values from -3 to 3
Outputs:
- new_pair: float32 [16, 128, 128, 128], P('crop', 'dap')
- input_grad: float32 [16, 128, 128, 128], P('crop', 'dap')
- grad_gain: float32 [2, 128], replicated
- grad_shift: float32 [2, 128], replicated
- grad_proj: float32 [2, 4, 128, 128], replicated
- grad_bias: float32 [2, 4, 128], replicated
- grad_gate: float32 [2, 128], replicated
- grad_out: float32 [2, 128, 128], replicated
- grad_outshift: float32 [2, 128], replicated
The draws below stay inside these ranges and needn't reach their ends.
All inputs are finite; a program needn't handle non-finite values.
Results may differ from the reference program's by a relative error of at most 0.00011.
Values sent between devices are 32-bit elements; how exact they have to be, the bound alone decides.
A program may use at most 64 MiB of HBM per device.

```python
import jax
import jax.numpy as jnp
from jax import lax

C = 128
HEADS = 4
N = 128
CROPS = 16


def block_levels(stream_key, dims, cuts, low, largest):
    level, own = 1.0, jax.random.fold_in(stream_key, 6)
    for axis_at, parts in cuts:
        draws = jnp.exp(jax.random.uniform(jax.random.fold_in(own, axis_at), (parts,), jnp.float32, low / len(cuts), largest / len(cuts)))
        level = level * jnp.repeat(draws, dims[axis_at] // parts).reshape([-1 if axis == axis_at else 1 for axis in range(len(dims))])
    return level


def centred(stream_key, shape, scale, most, cuts=(), kind=jnp.bfloat16):
    drawn = jax.random.normal(stream_key, shape, jnp.float32) * scale
    if len(cuts) > 0:
        drawn = block_levels(stream_key, shape, cuts, -0.22, 0.18) * drawn
    return jnp.clip(drawn, min=-most, max=most).astype(kind)


def setup_inputs(seed: int = 0) -> dict:
    key_of = jax.random.split(jax.random.key(seed), 10)
    pair = centred(key_of[0], (CROPS, N, N, C), 1.0, 6.0, ((0, 16), (1, 32)), jnp.float32)
    pair_grad = centred(key_of[1], (CROPS, N, N, C), 1.0, 6.0, ((0, 16), (1, 32)), jnp.float32)
    norm_gain = jnp.clip(1.0 + 0.1 * jax.random.normal(key_of[2], (2, C), jnp.float32), 0.5, 1.5)
    norm_shift = centred(key_of[3], (2, C), 0.5, 3.0, (), jnp.float32)
    proj_weight = centred(key_of[4], (2, 4, C, C), C ** -0.5, 0.5, (), jnp.float32)
    bias_weight = centred(key_of[5], (2, HEADS, C), C ** -0.5, 0.5, (), jnp.float32)
    gate_shift = centred(key_of[6], (2, C), 1.0, 4.0, (), jnp.float32)
    out_weight = centred(key_of[7], (2, C, C), C ** -0.5, 0.5, (), jnp.float32)
    out_shift = centred(key_of[8], (2, C), 0.5, 3.0, (), jnp.float32)
    return {"pair": pair, "pair_grad": pair_grad, "norm_gain": norm_gain, "norm_shift": norm_shift, "proj_weight": proj_weight, "bias_weight": bias_weight, "gate_shift": gate_shift, "out_weight": out_weight, "out_shift": out_shift}


EPSILON = 1e-05
HIGHEST = lax.Precision.HIGHEST

def layer_norm(field, gain, shift):
    center = field - lax.optimization_barrier(jnp.mean(field, axis=-1, keepdims=True))
    spread = lax.optimization_barrier(jnp.mean(center * center, axis=-1, keepdims=True))
    return center * lax.rsqrt(spread + EPSILON) * gain + shift

def project(pair_rows, gain, shift, weights, bias_proj):
    normed = layer_norm(pair_rows, gain, shift)
    stacked = jnp.einsum('ijc,gcd->gijd', normed, weights, precision=HIGHEST)
    bias_rows = jnp.einsum('ijc,hc->hij', normed, bias_proj, precision=HIGHEST)
    return (stacked, bias_rows)

def attend(stacked, bias_full, gate_bias, out_proj, out_bias):
    row_count, col_count, channels = (stacked.shape[1], stacked.shape[2], stacked.shape[3])
    head_size = channels // HEADS
    shape = (row_count, col_count, HEADS, head_size)
    queries = stacked[0].reshape(shape) * head_size ** (-0.5)
    key_rows = stacked[1].reshape(shape)
    value_rows = stacked[2].reshape(shape)
    scores = jnp.einsum('ijhd,ikhd->ihjk', queries, key_rows, precision=HIGHEST) + bias_full[None]
    probs = jax.nn.softmax(scores, axis=-1)
    attended = jnp.einsum('ihjk,ikhd->ijhd', probs, value_rows, precision=HIGHEST).reshape(row_count, col_count, channels)
    gated_out = jax.nn.sigmoid(stacked[3] + gate_bias) * attended
    return jnp.einsum('ijc,cd->ijd', gated_out, out_proj, precision=HIGHEST) + out_bias

def update(field, params, which):
    member = tuple((entry[which] for entry in params))
    stacked, bias_full = project(field, *member[:4])
    return attend(stacked, bias_full, *member[4:])

def forward(field, *params):
    middle = field + update(field, params, 0)
    swapped = jnp.swapaxes(middle, 0, 1)
    return middle + jnp.swapaxes(update(swapped, params, 1), 0, 1)

def reference(pair, pair_grad, norm_gain, norm_shift, proj_weight, bias_weight, gate_shift, out_weight, out_shift):
    params = (norm_gain, norm_shift, proj_weight, bias_weight, gate_shift, out_weight, out_shift)

    def per_crop(inputs):
        crop_pair, crop_grad = inputs
        final, back = jax.vjp(forward, crop_pair, *params)
        grads = back(crop_grad)
        return (final, grads[0], grads[1:])
    new_pair, input_grad, grads = lax.map(per_crop, (pair, pair_grad))
    scale = 1.0 / (CROPS * N)
    totals = tuple((lax.optimization_barrier(jnp.sum(entry, axis=0)) * scale for entry in grads))
    return (new_pair, input_grad, totals[0], totals[1], totals[2], totals[3], totals[4], totals[5], totals[6])
```

```python
import functools

import jax
import jax.numpy as jnp
from jax import lax
from jax.experimental import pallas as pl
from jax.experimental.pallas import tpu as pltpu
from jax.sharding import PartitionSpec as P

HEADS = 4
EPSILON = 1e-05
F32 = jnp.float32
BF16 = jnp.bfloat16
MESH = pl.DeviceIdType.MESH
NN = (((1,), (0,)), ((), ()))
NT = (((1,), (1,)), ((), ()))
Z = 16


def split(x):
    hi = x.astype(BF16)
    return hi, (x - hi.astype(F32)).astype(BF16)


def dot(a, b, dims):
    return lax.dot_general(a, b, dims, preferred_element_type=F32)


def dot3(a, b, dims):
    return dot(a[0], b[0], dims) + (dot(a[0], b[1], dims) + dot(a[1], b[0], dims))


def dot3m(a, b, dims):
    rows = a[0].shape[0]
    both = dot(jnp.concatenate(a, axis=0), b[0], dims)
    return both[:rows] + (both[rows:] + dot(a[0], b[1], dims))


def dot_tn(a, b):
    ah, al = split(a)
    bh, bl = split(b)
    stacked = jnp.concatenate([ah.astype(F32), ah.astype(F32), al.astype(F32), al.astype(F32)], axis=0)
    return dot(stacked.T.astype(BF16), jnp.concatenate([bh, bl, bh, bl], axis=0), NN)


def normalise(z):
    center = z - jnp.mean(z, axis=-1, keepdims=True)
    spread = jnp.mean(center * center, axis=-1, keepdims=True)
    r = lax.rsqrt(spread + EPSILON)
    return center * r, r


def normalise_back(dn, n, r):
    first = jnp.mean(dn, axis=-1, keepdims=True)
    second = jnp.mean(dn * n, axis=-1, keepdims=True)
    return r * (dn - first - n * second)


def kernel(
    D,
    NC,
    pair_ref, grad_ref, gain_ref, shift_ref, w_ref, bw_ref, gs_ref, wo_ref, os_ref,
    new_ref, igrad_ref, ggain_ref, gshift_ref, gproj_ref, gbias_ref, ggate_ref, gout_ref, gos_ref,
    z_ref, n_ref, r_ref, nm_ref, rm_ref, up_ref, mg_ref, dxt_ref,
    wt_ref, xt_ref, pt_ref, at_ref, ot_ref, yt_ref, dot_ref, dpt_ref, bt_ref, db_ref,
    stage_ref, chunk_ref, recv_ref,
    big_ref, bigr_ref, msg_ref, near_ref, far_ref, last_ref, tiny_ref,
    send_sem, recv_sem, wsend_sem, wrecv_sem,
):
    R = 4
    N = R * D
    T = R * N
    C = 128
    HS = C // HEADS
    scale = HS ** (-0.5)
    out_scale = 1.0 / (NC * N)
    me = lax.axis_index("dap")
    crop = lax.axis_index("crop")
    Y = D // Z if D >= Z else 1
    z_len = D // Y
    y_at, z_at = me // z_len, lax.rem(me, z_len)
    near_len, far_len = 4 * Y, z_len // 4
    block, inner = z_at // 4, lax.rem(z_at, 4)
    near_me = y_at * 4 + inner

    barrier = pltpu.get_barrier_semaphore()

    @pl.loop(1, D)
    def _(s):
        pl.semaphore_signal(barrier, inc=1, device_id=(crop, lax.rem(me + s, D)), device_id_type=MESH)

    @pl.loop(1, NC)
    def _(s):
        pl.semaphore_signal(barrier, inc=1, device_id=(lax.rem(crop + s, NC), me), device_id_type=MESH)

    def copy_to(src, dst, sems, k, device):
        return pltpu.make_async_remote_copy(
            src_ref=src, dst_ref=dst, send_sem=sems[0].at[k], recv_sem=sems[1].at[k],
            device_id=device, device_id_type=MESH)

    dap_sems = (send_sem, recv_sem)
    w_sems = (wsend_sem, wrecv_sem)

    def send_all(k, slot):
        @pl.loop(1, D)
        def _(s):
            peer = lax.rem(me + s, D)
            copy_to(stage_ref.at[slot, peer], recv_ref.at[k, me], dap_sems, k, (crop, peer)).start()
        recv_ref[k, me] = stage_ref[slot, me]

    def send_same(k, slot):
        @pl.loop(1, D)
        def _(s):
            peer = lax.rem(me + s, D)
            copy_to(chunk_ref.at[slot], recv_ref.at[k, me], dap_sems, k, (crop, peer)).start()
        recv_ref[k, me] = chunk_ref[slot]

    def wait_bytes(ref, sem):
        pltpu.make_async_copy(ref, ref, sem).wait()

    def arrived(k):
        wait_bytes(recv_ref.at[k, pl.ds(0, D - 1)], recv_sem.at[k])

    def put_stage(slot, row, tile):
        stage_ref[slot, :, row, :] = tile

    def get_recv(k, row):
        return recv_ref[k, :, row, :]

    for i in range(R):
        for j in range(R):
            at = (i * R + j) * D
            z_ref[0, at:at + D] = pair_ref[pl.ds(i * N + j, D, stride=R)]
            tile = grad_ref[pl.ds(i * N + j, D, stride=R)]
            up_ref[at:at + D] = tile
            put_stage(0, i * R + j, tile)

    def prepare(b):
        for g in range(4):
            w = w_ref[b, g]
            if g == 0:
                w = w * scale
            hi, lo = split(w.T)
            wt_ref[b, 0, g * C:(g + 1) * C] = hi
            wt_ref[b, 1, g * C:(g + 1) * C] = lo

    def columns(b):
        rows = jnp.concatenate([gs_ref[b:b + 1], jnp.zeros((7, C), F32)], axis=0)
        return rows.T[:, 0:1]

    def bias_rows(b, x_split):
        bw = jnp.concatenate([bw_ref[b], jnp.zeros((4, C), F32)], axis=0)
        return dot3m(split(bw), x_split, NN)

    def put_chunk(slot, rows):
        for i in range(R):
            chunk_ref[slot, i * HEADS:(i + 1) * HEADS] = rows[0:HEADS, i * N:(i + 1) * N]

    def project(b, x_split):
        out = dot3((wt_ref[b, 0], wt_ref[b, 1]), x_split, NN)
        out_gate = jax.nn.sigmoid(out[3 * C:] + columns(b))
        for i in range(R):
            pt_ref[b, i, 0:3 * C] = out[0:3 * C, i * N:(i + 1) * N]
            pt_ref[b, i, 3 * C:] = out_gate[:, i * N:(i + 1) * N]

    def attend(b):
        @pl.loop(0, R)
        def _(i):
            for h in range(HEADS):
                at = h * HS
                q = pt_ref[b, i, at:at + HS]
                k = pt_ref[b, i, C + at:C + at + HS]
                v = pt_ref[b, i, 2 * C + at:2 * C + at + HS]
                s = dot_tn(k, q) + bt_ref[b, h]
                e = jnp.exp(s - jnp.max(s, axis=0, keepdims=True))
                a = e * (1.0 / jnp.sum(e, axis=0, keepdims=True))
                at_ref[b, i, h] = a
                o = dot3m(split(v), split(a), NN)
                ot_ref[b, i, at:at + HS] = o
                yt_ref[b, i, at:at + HS] = o * pt_ref[b, i, 3 * C + at:3 * C + at + HS]

    def over_rows(ref, b):
        return jnp.concatenate([ref[b, i] for i in range(R)], axis=1)

    def update(b):
        y = split(over_rows(yt_ref, b))
        ut = dot3(split(wo_ref[b].T), y, NN)
        return ut.T + os_ref[b:b + 1]

    def backward(b, du, put_bias_grad):
        du_split = split(du)
        dyt = dot3(split(wo_ref[b]), du_split, NT)
        for i in range(R):
            dy = dyt[:, i * N:(i + 1) * N]
            gate = pt_ref[b, i, 3 * C:]
            dot_ref[i] = dy * gate
            dpt_ref[b, i, 3 * C:] = dy * ot_ref[b, i] * (gate * (1.0 - gate))
        db_ref[b] = jnp.zeros((HEADS, N, N), F32)

        @pl.loop(0, R)
        def _(i):
            for h in range(HEADS):
                at = h * HS
                q = pt_ref[b, i, at:at + HS]
                k = pt_ref[b, i, C + at:C + at + HS]
                v = pt_ref[b, i, 2 * C + at:2 * C + at + HS]
                a = at_ref[b, i, h]
                do = dot_ref[i, at:at + HS]
                row = jnp.sum(do * ot_ref[b, i, at:at + HS], axis=0, keepdims=True)
                ds = a * (dot_tn(v, do) - row)
                db_ref[b, h] += ds
                ds_split = split(ds)
                dpt_ref[b, i, at:at + HS] = dot3m(split(k), ds_split, NN)
                dpt_ref[b, i, C + at:C + at + HS] = dot3m(split(q), ds_split, NT)
                dpt_ref[b, i, 2 * C + at:2 * C + at + HS] = dot3m(split(do), split(a), NT)
        put_bias_grad()
        return du_split

    def dx_local(b):
        total = None
        for g in range(4):
            w = w_ref[b, g]
            if g == 0:
                w = w * scale
            d = jnp.concatenate([dpt_ref[b, i, g * C:(g + 1) * C] for i in range(R)], axis=1)
            term = dot3(split(w), split(d), NN)
            total = term if total is None else total + term
        return total

    def big_grads(b, x_split, du_split):
        rows = 5 * C // NC
        parts = []
        for g in range(4):
            d = jnp.concatenate([dpt_ref[b, i, g * C:(g + 1) * C] for i in range(R)], axis=1)
            out = dot3(x_split, split(d), NT)
            parts.append(out * scale if g == 0 else out)
        parts.append(dot3(split(over_rows(yt_ref, b)), du_split, NN))
        whole = jnp.concatenate(parts, axis=0)
        for p in range(NC):
            big_ref[b, p] = whole[p * rows:(p + 1) * rows]

    def send_big(b):
        @pl.loop(1, NC)
        def _(s):
            peer = lax.rem(crop + s, NC)
            copy_to(big_ref.at[b, peer], bigr_ref.at[b, crop], w_sems, 4 * b, (peer, me)).start()
        bigr_ref[b, crop] = big_ref[b, crop]

    def send_near(b):
        wait_bytes(bigr_ref.at[b, pl.ds(0, NC - 1)], wrecv_sem.at[4 * b])
        rows = 5 * C // NC
        total = bigr_ref[b, 0]
        for p in range(1, NC):
            total = total + bigr_ref[b, p]
        msg_ref[b, 0, 0:rows] = total
        msg_ref[b, 0, rows:rows + 8] = tiny_ref[b]

        @pl.loop(1, near_len)
        def _(s):
            m = lax.rem(near_me + s, near_len)
            peer = (m // 4) * z_len + block * 4 + lax.rem(m, 4)
            copy_to(msg_ref.at[b, 0], near_ref.at[b, near_me], w_sems, 4 * b + 1, (crop, peer)).start()
        near_ref[b, near_me] = msg_ref[b, 0]

    def send_far(b):
        wait_bytes(near_ref.at[b, pl.ds(0, near_len - 1)], wrecv_sem.at[4 * b + 1])
        total = near_ref[b, 0]
        for p in range(1, near_len):
            total = total + near_ref[b, p]
        msg_ref[b, 1] = total

        @pl.loop(1, far_len)
        def _(s):
            m = lax.rem(block + s, far_len)
            peer = y_at * z_len + m * 4 + inner
            copy_to(msg_ref.at[b, 1], far_ref.at[b, block], w_sems, 4 * b + 2, (crop, peer)).start()
        far_ref[b, block] = msg_ref[b, 1]

    def send_last(b):
        wait_bytes(far_ref.at[b, pl.ds(0, far_len - 1)], wrecv_sem.at[4 * b + 2])
        total = far_ref[b, 0]
        for p in range(1, far_len):
            total = total + far_ref[b, p]
        msg_ref[b, 2] = total * out_scale

        @pl.loop(1, NC)
        def _(s):
            peer = lax.rem(crop + s, NC)
            copy_to(msg_ref.at[b, 2], last_ref.at[b, crop], w_sems, 4 * b + 3, (peer, me)).start()
        last_ref[b, crop] = msg_ref[b, 2]

    def finish_big(b):
        wait_bytes(last_ref.at[b, pl.ds(0, NC - 1)], wrecv_sem.at[4 * b + 3])
        rows = 5 * C // NC
        for p in range(NC):
            first = p * rows
            while first < (p + 1) * rows:
                g, at = first // C, first % C
                count = min((p + 1) * rows - first, C - at)
                piece = last_ref[b, p, first - p * rows:first - p * rows + count]
                if g < 4:
                    gproj_ref[b, g, at:at + count] = piece
                else:
                    gout_ref[b, at:at + count] = piece
                first += count
        tiny = last_ref[b, 0, rows:rows + 8]
        for p in range(1, NC):
            tiny = tiny + last_ref[b, p, rows:rows + 8]
        ggain_ref[b:b + 1] = tiny[0:1]
        gshift_ref[b:b + 1] = tiny[1:2]
        gbias_ref[b] = tiny[2:2 + HEADS]
        ggate_ref[b:b + 1] = tiny[6:7]
        gos_ref[b:b + 1] = tiny[7:8]

    def gate_grad(b):
        total = None
        for i in range(R):
            d = dpt_ref[b, i, 3 * C:]
            total = d if total is None else total + d
        return jnp.sum(total.T, axis=0, keepdims=True)

    def bias_grad(k):
        total = recv_ref[k, 0]
        for p in range(1, D):
            total = total + recv_ref[k, p]
        rows = jnp.concatenate([total[i * HEADS:(i + 1) * HEADS] for i in range(R)], axis=1)
        return jnp.concatenate([rows, jnp.zeros((4, T), F32)], axis=0)

    def bias_part(b, dbr, x_split):
        bw = jnp.concatenate([bw_ref[b], jnp.zeros((4, C), F32)], axis=0)
        d_split = split(dbr)
        dxt = dot3(split(bw.T), d_split, NN)
        dbw = dot3m(d_split, x_split, NT)
        return dxt, dbw[0:HEADS]

    def col_sum(x):
        return jnp.sum(x, axis=0, keepdims=True)

    n0, r0 = normalise(z_ref[0])
    n_ref[0] = n0
    r_ref[0] = r0
    x0_split = split((n0 * gain_ref[0:1] + shift_ref[0:1]).T)
    xt_ref[0, 0] = x0_split[0]
    xt_ref[0, 1] = x0_split[1]
    put_chunk(0, bias_rows(0, x0_split))
    pl.semaphore_wait(barrier, D - 1 + NC - 1)
    send_same(0, 0)
    send_all(1, 0)
    prepare(0)
    prepare(1)
    project(0, x0_split)
    arrived(0)
    for h in range(HEADS):
        bt_ref[0, h] = jnp.concatenate([get_recv(0, i * HEADS + h) for i in range(R)], axis=0).T
    attend(0)
    z_ref[1] = z_ref[0] + update(0)

    for row in range(R * R):
        put_stage(1, row, z_ref[1, row * D:(row + 1) * D])
    send_all(2, 1)
    nm, rm = normalise(z_ref[1])
    nm_ref[...] = nm
    rm_ref[...] = rm
    xm_split = split((nm * gain_ref[1:2] + shift_ref[1:2]).T)
    xt_ref[2, 0] = xm_split[0]
    xt_ref[2, 1] = xm_split[1]
    put_chunk(1, bias_rows(1, xm_split))
    send_same(3, 1)

    arrived(2)

    def columns_layout(k):
        return jnp.concatenate([get_recv(k, i * R + j) for j in range(R) for i in range(R)], axis=0)

    n1, r1 = normalise(columns_layout(2))
    n_ref[1] = n1
    r_ref[1] = r1
    x1_split = split((n1 * gain_ref[1:2] + shift_ref[1:2]).T)
    xt_ref[1, 0] = x1_split[0]
    xt_ref[1, 1] = x1_split[1]
    project(1, x1_split)
    arrived(3)
    for h in range(HEADS):
        bt_ref[1, h] = jnp.concatenate([get_recv(3, i * HEADS + h) for i in range(R)], axis=0)
    attend(1)
    u1 = update(1)

    def stage_back(slot, value):
        for j in range(R):
            for i in range(R):
                at = (j * R + i) * D
                put_stage(slot, i * R + j, value[at:at + D])

    stage_back(2, u1)

    arrived(1)
    du1 = columns_layout(1)

    def bias_grad_1():
        for h in range(HEADS):
            for i in range(R):
                put_stage(3, i * HEADS + h, db_ref[1, h, i * D:(i + 1) * D])
        send_all(5, 3)

    du1_split = backward(1, du1, bias_grad_1)
    dx1 = dx_local(1).T
    stage_back(4, normalise_back(dx1 * gain_ref[1:2], n_ref[1], r_ref[1]))
    send_all(6, 4)
    send_all(4, 2)
    big_grads(1, (xt_ref[1, 0], xt_ref[1, 1]), du1_split)
    send_big(1)
    tiny_ref[1, 0:1] = col_sum(dx1 * n_ref[1])
    tiny_ref[1, 1:2] = col_sum(dx1)
    tiny_ref[1, 6:7] = gate_grad(1)
    tiny_ref[1, 7:8] = col_sum(du1)
    arrived(5)
    dxm_t, dbw1 = bias_part(1, bias_grad(5), (xt_ref[2, 0], xt_ref[2, 1]))
    dxm = dxm_t.T
    tiny_ref[1, 0:1] += col_sum(dxm * nm_ref[...])
    tiny_ref[1, 1:2] += col_sum(dxm)
    tiny_ref[1, 2:2 + HEADS] = dbw1
    send_near(1)
    mg_ref[...] = up_ref[...] + normalise_back(dxm * gain_ref[1:2], nm_ref[...], rm_ref[...])
    arrived(6)
    for row in range(R * R):
        mg_ref[row * D:(row + 1) * D] += get_recv(6, row)

    def bias_grad_0():
        for h in range(HEADS):
            turned = db_ref[0, h].T
            for i in range(R):
                put_stage(5, i * HEADS + h, turned[i * D:(i + 1) * D])
        send_all(7, 5)

    du0_split = backward(0, mg_ref[...], bias_grad_0)
    big_grads(0, (xt_ref[0, 0], xt_ref[0, 1]), du0_split)
    send_big(0)
    send_far(1)
    tiny_ref[0, 6:7] = gate_grad(0)
    tiny_ref[0, 7:8] = col_sum(mg_ref[...])
    dxt_ref[...] = dx_local(0)
    arrived(4)
    for i in range(R):
        for j in range(R):
            row = i * R + j
            new_ref[pl.ds(i * N + j, D, stride=R)] = z_ref[1, row * D:(row + 1) * D] + get_recv(4, row)
    arrived(7)
    dx0_t, dbw0 = bias_part(0, bias_grad(7), (xt_ref[0, 0], xt_ref[0, 1]))
    dx0 = (dxt_ref[...] + dx0_t).T
    tiny_ref[0, 0:1] = col_sum(dx0 * n_ref[0])
    tiny_ref[0, 1:2] = col_sum(dx0)
    tiny_ref[0, 2:2 + HEADS] = dbw0
    send_near(0)
    send_last(1)
    dz0 = normalise_back(dx0 * gain_ref[0:1], n_ref[0], r_ref[0])
    for i in range(R):
        for j in range(R):
            at = (i * R + j) * D
            igrad_ref[pl.ds(i * N + j, D, stride=R)] = mg_ref[at:at + D] + dz0[at:at + D]
    send_far(0)
    finish_big(1)
    send_last(0)
    finish_big(0)

    for k in range(8):
        wait_bytes(recv_ref.at[k, pl.ds(0, D - 1)], send_sem.at[k])
    for b in range(2):
        wait_bytes(bigr_ref.at[b, pl.ds(0, NC - 1)], wsend_sem.at[4 * b])
        wait_bytes(near_ref.at[b, pl.ds(0, near_len - 1)], wsend_sem.at[4 * b + 1])
        if far_len > 1:
            wait_bytes(far_ref.at[b, pl.ds(0, far_len - 1)], wsend_sem.at[4 * b + 2])
        wait_bytes(last_ref.at[b, pl.ds(0, NC - 1)], wsend_sem.at[4 * b + 3])


def body(D, NC, pair, pair_grad, gain, shift, w, bw, gs, wo, os):
    R, N, C = pair.shape[1:]
    T = R * N
    Y = D // Z
    rows = 5 * C // NC
    vmem = pl.BlockSpec(memory_space=pltpu.VMEM)
    out = lambda *shape: jax.ShapeDtypeStruct(shape, F32)
    results = pl.pallas_call(
        functools.partial(kernel, D, NC),
        out_shape=[out(T, C), out(T, C), out(2, C), out(2, C), out(2, 4, C, C), out(2, HEADS, C), out(2, C),
                   out(2, C, C), out(2, C)],
        in_specs=[vmem] * 9,
        out_specs=[vmem] * 9,
        scratch_shapes=[
            pltpu.VMEM((2, T, C), F32),
            pltpu.VMEM((2, T, C), F32),
            pltpu.VMEM((2, T, 1), F32),
            pltpu.VMEM((T, C), F32),
            pltpu.VMEM((T, 1), F32),
            pltpu.VMEM((T, C), F32),
            pltpu.VMEM((T, C), F32),
            pltpu.VMEM((C, T), F32),
            pltpu.VMEM((2, 2, 4 * C, C), BF16),
            pltpu.VMEM((3, 2, C, T), BF16),
            pltpu.VMEM((2, R, 4 * C, N), F32),
            pltpu.VMEM((2, R, HEADS, N, N), F32),
            pltpu.VMEM((2, R, C, N), F32),
            pltpu.VMEM((2, R, C, N), F32),
            pltpu.VMEM((R, C, N), F32),
            pltpu.VMEM((2, R, 4 * C, N), F32),
            pltpu.VMEM((2, HEADS, N, N), F32),
            pltpu.VMEM((2, HEADS, N, N), F32),
            pltpu.VMEM((6, D, R * R, C), F32),
            pltpu.VMEM((2, R * R, N), F32),
            pltpu.VMEM((8, D, R * R, C), F32),
            pltpu.VMEM((2, NC, rows, C), F32),
            pltpu.VMEM((2, NC, rows, C), F32),
            pltpu.VMEM((2, 3, rows + 8, C), F32),
            pltpu.VMEM((2, 4 * Y, rows + 8, C), F32),
            pltpu.VMEM((2, Z // 4, rows + 8, C), F32),
            pltpu.VMEM((2, NC, rows + 8, C), F32),
            pltpu.VMEM((2, 8, C), F32),
            pltpu.SemaphoreType.DMA((8,)),
            pltpu.SemaphoreType.DMA((8,)),
            pltpu.SemaphoreType.DMA((8,)),
            pltpu.SemaphoreType.DMA((8,)),
        ],
        compiler_params=pltpu.CompilerParams(
            collective_id=0, has_side_effects=True, vmem_limit_bytes=56 * 1024 * 1024),
    )(pair.reshape(T, C), pair_grad.reshape(T, C), gain, shift, w, bw, gs, wo, os)
    return (results[0].reshape(pair.shape), results[1].reshape(pair.shape)) + tuple(results[2:])


def solution(mesh):
    rows = P("crop", "dap", None, None)
    return jax.shard_map(
        functools.partial(body, mesh.shape["dap"], mesh.shape["crop"]),
        mesh=mesh,
        in_specs=(rows, rows) + (P(),) * 7,
        out_specs=(rows, rows) + (P(),) * 7,
        check_vma=False,
    )
```

```python
import functools

import jax
import jax.numpy as jnp
from jax import lax
from jax.experimental import pallas as pl
from jax.experimental.pallas import tpu as pltpu
from jax.sharding import PartitionSpec as P

HEADS = 4
EPSILON = 1e-05
F32 = jnp.float32
BF16 = jnp.bfloat16
MESH = pl.DeviceIdType.MESH
NN = (((1,), (0,)), ((), ()))
NT = (((1,), (1,)), ((), ()))
Z = 16


def split(x):
    hi = x.astype(BF16)
    return hi, (x - hi.astype(F32)).astype(BF16)


def dot(a, b, dims):
    return lax.dot_general(a, b, dims, preferred_element_type=F32)


def dot3(a, b, dims):
    return dot(a[0], b[0], dims) + (dot(a[0], b[1], dims) + dot(a[1], b[0], dims))


def dot3m(a, b, dims):
    rows = a[0].shape[0]
    both = dot(jnp.concatenate(a, axis=0), b[0], dims)
    return both[:rows] + (both[rows:] + dot(a[0], b[1], dims))


def dot_tn(a, b):
    ah, al = split(a)
    bh, bl = split(b)
    stacked = jnp.concatenate([ah.astype(F32), ah.astype(F32), al.astype(F32), al.astype(F32)], axis=0)
    return dot(stacked.T.astype(BF16), jnp.concatenate([bh, bl, bh, bl], axis=0), NN)


def normalise(z):
    center = z - jnp.mean(z, axis=-1, keepdims=True)
    spread = jnp.mean(center * center, axis=-1, keepdims=True)
    r = lax.rsqrt(spread + EPSILON)
    return center * r, r


def normalise_back(dn, n, r):
    first = jnp.mean(dn, axis=-1, keepdims=True)
    second = jnp.mean(dn * n, axis=-1, keepdims=True)
    return r * (dn - first - n * second)


def kernel(
    D,
    NC,
    pair_ref, grad_ref, gain_ref, shift_ref, w_ref, bw_ref, gs_ref, wo_ref, os_ref,
    new_ref, igrad_ref, ggain_ref, gshift_ref, gproj_ref, gbias_ref, ggate_ref, gout_ref, gos_ref,
    z_ref, n_ref, r_ref, nm_ref, rm_ref, up_ref, mg_ref, dx_ref, dxt_ref,
    wt_ref, xt_ref, pt_ref, at_ref, ot_ref, yt_ref, dot_ref, dpt_ref, bt_ref, db_ref,
    stage_ref, chunk_ref, recv_ref, gather_ref, pairsum_ref, zstage_ref, zrecv_ref,
    big_ref, bigr_ref, msg0_ref, msg1_ref, near0_ref, near1_ref, far0_ref, far1_ref, last0_ref, last1_ref,
    tiny_ref, tinyz_ref, tinyp_ref,
    send_sem, recv_sem,
):
    R = 4
    N = R * D
    T = R * N
    C = 128
    HS = C // HEADS
    scale = HS ** (-0.5)
    out_scale = 1.0 / (NC * N)
    me = lax.axis_index("dap")
    crop = lax.axis_index("crop")
    y_at, z_at = me // Z, lax.rem(me, Z)
    block, inner = z_at // 4, lax.rem(z_at, 4)
    NP = 2 * NC
    plane_me = crop * 2 + y_at
    rows = 5 * C // NP

    barrier = pltpu.get_barrier_semaphore()

    def plane_device(p):
        return (p // 2, lax.rem(p, 2) * Z + z_at)

    def z_device(z):
        return (crop, y_at * Z + z)

    partner = (crop, (1 - y_at) * Z + z_at)

    @pl.loop(1, D)
    def _(s):
        pl.semaphore_signal(barrier, inc=1, device_id=(crop, lax.rem(me + s, D)), device_id_type=MESH)

    @pl.loop(1, NP)
    def _(s):
        pl.semaphore_signal(barrier, inc=1, device_id=plane_device(lax.rem(plane_me + s, NP)), device_id_type=MESH)

    def copy_to(src, dst, k, device):
        return pltpu.make_async_remote_copy(
            src_ref=src, dst_ref=dst, send_sem=send_sem.at[k], recv_sem=recv_sem.at[k],
            device_id=device, device_id_type=MESH)

    def wait_bytes(ref, sem):
        pltpu.make_async_copy(ref, ref, sem).wait()

    sent = []

    def arrived(k, ref):
        wait_bytes(ref, recv_sem.at[k])
        sent.append((k, ref))

    def send_half(x, m):
        k = 2 * x + m
        part = pl.ds(8 * m, 8)

        def to(y, z):
            peer = lax.rem(y, 2) * Z + lax.rem(z, Z)
            copy_to(stage_ref.at[x, peer, part], recv_ref.at[x, me, part], k, (crop, peer)).start()

        to(y_at, z_at + 8)
        to(y_at + 1, z_at + 8)

        @pl.loop(1, 8)
        def _(s):
            to(y_at, z_at + 8 - s)
            to(y_at, z_at + 8 + s)
            to(y_at + 1, z_at + 8 - s)
            to(y_at + 1, z_at + 8 + s)

        to(y_at + 1, z_at)
        recv_ref[x, me, part] = stage_ref[x, me, part]

    def half_arrived(x, m):
        arrived(2 * x + m, recv_ref.at[x, pl.ds(0, D - 1), pl.ds(8 * m, 8)])

    def gather_z(g):
        def to(z, k):
            copy_to(chunk_ref.at[g], gather_ref.at[g, me], k, z_device(lax.rem(z, Z))).start()

        @pl.loop(0, 7)
        def _(s):
            to(z_at + 5 + s, 9 + 3 * g)

        @pl.loop(0, 8)
        def _(s):
            to(z_at + 12 + s + s // 4, 8 + 3 * g)

        gather_ref[g, me] = chunk_ref[g]

    def forward(g, z):
        slot = y_at * Z + lax.rem(z, Z)
        copy_to(gather_ref.at[g, slot], gather_ref.at[g, slot], 10 + 3 * g, partner).start()

    def forward_near(g):
        forward(g, z_at)
        arrived(8 + 3 * g, gather_ref.at[g, pl.ds(0, 8)])

        @pl.loop(0, 8)
        def _(s):
            forward(g, z_at + 12 + s + s // 4)

    def forward_far(g):
        arrived(9 + 3 * g, gather_ref.at[g, pl.ds(0, 7)])

        @pl.loop(0, 7)
        def _(s):
            forward(g, z_at + 5 + s)

    def gathered(g):
        arrived(10 + 3 * g, gather_ref.at[g, pl.ds(0, Z)])

    def reduce_y(g):
        copy_to(stage_ref.at[4 + g, pl.ds((1 - y_at) * Z, Z)], pairsum_ref.at[g], 14 + 2 * g, partner).start()

    def reduce_z(g):
        arrived(14 + 2 * g, pairsum_ref.at[g])
        zstage_ref[g] = stage_ref[4 + g, pl.ds(y_at * Z, Z)] + pairsum_ref[g]

        @pl.loop(1, Z)
        def _(s):
            z = lax.rem(z_at + s, Z)
            copy_to(zstage_ref.at[g, z], zrecv_ref.at[g, z_at], 15 + 2 * g, z_device(z)).start()

        zrecv_ref[g, z_at] = zstage_ref[g, z_at]

    def reduced(g):
        arrived(15 + 2 * g, zrecv_ref.at[g, pl.ds(0, Z - 1)])
        total = zrecv_ref[g, 0]
        for p in range(1, Z):
            total = total + zrecv_ref[g, p]
        whole = jnp.concatenate([total[i * HEADS:(i + 1) * HEADS] for i in range(R)], axis=1)
        return jnp.concatenate([whole, jnp.zeros((4, T), F32)], axis=0)

    def put_stage(slot, row, tile):
        stage_ref[slot, :, row, :] = tile

    def get_recv(x, row):
        return recv_ref[x, :, row, :]

    for i in range(R):
        for j in range(R):
            at = (i * R + j) * D
            z_ref[0, at:at + D] = pair_ref[pl.ds(i * N + j, D, stride=R)]
            tile = grad_ref[pl.ds(i * N + j, D, stride=R)]
            up_ref[at:at + D] = tile
            put_stage(0, i * R + j, tile)

    def prepare(b):
        for g in range(4):
            w = w_ref[b, g]
            if g == 0:
                w = w * scale
            hi, lo = split(w.T)
            wt_ref[b, 0, g * C:(g + 1) * C] = hi
            wt_ref[b, 1, g * C:(g + 1) * C] = lo

    def columns(b):
        rows = jnp.concatenate([gs_ref[b:b + 1], jnp.zeros((7, C), F32)], axis=0)
        return rows.T[:, 0:1]

    def bias_rows(b, x_split):
        bw = jnp.concatenate([bw_ref[b], jnp.zeros((4, C), F32)], axis=0)
        return dot3m(split(bw), x_split, NN)

    def put_chunk(slot, rows):
        for i in range(R):
            chunk_ref[slot, i * HEADS:(i + 1) * HEADS] = rows[0:HEADS, i * N:(i + 1) * N]

    def project(b, x_split):
        out = dot3((wt_ref[b, 0], wt_ref[b, 1]), x_split, NN)
        out_gate = jax.nn.sigmoid(out[3 * C:] + columns(b))
        for i in range(R):
            pt_ref[b, i, 0:3 * C] = out[0:3 * C, i * N:(i + 1) * N]
            pt_ref[b, i, 3 * C:] = out_gate[:, i * N:(i + 1) * N]

    def attend(b, lo, hi):
        @pl.loop(lo, hi)
        def _(i):
            for h in range(HEADS):
                at = h * HS
                q = pt_ref[b, i, at:at + HS]
                k = pt_ref[b, i, C + at:C + at + HS]
                v = pt_ref[b, i, 2 * C + at:2 * C + at + HS]
                s = dot_tn(k, q) + bt_ref[b, h]
                e = jnp.exp(s - jnp.max(s, axis=0, keepdims=True))
                a = e * (1.0 / jnp.sum(e, axis=0, keepdims=True))
                at_ref[b, i, h] = a
                o = dot3m(split(v), split(a), NN)
                ot_ref[b, i, at:at + HS] = o
                yt_ref[b, i, at:at + HS] = o * pt_ref[b, i, 3 * C + at:3 * C + at + HS]

    def over_rows(ref, b, lo=0, hi=R):
        return jnp.concatenate([ref[b, i] for i in range(lo, hi)], axis=1)

    def update(b, lo, hi):
        ut = dot3(split(wo_ref[b].T), split(over_rows(yt_ref, b, lo, hi)), NN)
        return ut.T + os_ref[b:b + 1]

    def backward(b, du, put_bias_grad):
        du_split = split(du)
        dyt = dot3(split(wo_ref[b]), du_split, NT)
        for i in range(R):
            dy = dyt[:, i * N:(i + 1) * N]
            gate = pt_ref[b, i, 3 * C:]
            dot_ref[i] = dy * gate
            dpt_ref[b, i, 3 * C:] = dy * ot_ref[b, i] * (gate * (1.0 - gate))
        db_ref[b] = jnp.zeros((HEADS, N, N), F32)

        @pl.loop(0, R)
        def _(i):
            for h in range(HEADS):
                at = h * HS
                q = pt_ref[b, i, at:at + HS]
                k = pt_ref[b, i, C + at:C + at + HS]
                v = pt_ref[b, i, 2 * C + at:2 * C + at + HS]
                a = at_ref[b, i, h]
                do = dot_ref[i, at:at + HS]
                row = jnp.sum(do * ot_ref[b, i, at:at + HS], axis=0, keepdims=True)
                ds = a * (dot_tn(v, do) - row)
                db_ref[b, h] += ds
                ds_split = split(ds)
                dpt_ref[b, i, at:at + HS] = dot3m(split(k), ds_split, NN)
                dpt_ref[b, i, C + at:C + at + HS] = dot3m(split(q), ds_split, NT)
                dpt_ref[b, i, 2 * C + at:2 * C + at + HS] = dot3m(split(do), split(a), NT)
        put_bias_grad()
        return du_split

    def dx_local(b, lo, hi):
        total = None
        for g in range(4):
            w = w_ref[b, g]
            if g == 0:
                w = w * scale
            d = jnp.concatenate([dpt_ref[b, i, g * C:(g + 1) * C] for i in range(lo, hi)], axis=1)
            term = dot3(split(w), split(d), NN)
            total = term if total is None else total + term
        return total

    msgs, nears, fars, lasts = (msg0_ref, msg1_ref), (near0_ref, near1_ref), (far0_ref, far1_ref), (last0_ref, last1_ref)

    def big_grads(b, x_split, du_split):
        parts = []
        for g in range(4):
            d = jnp.concatenate([dpt_ref[b, i, g * C:(g + 1) * C] for i in range(R)], axis=1)
            out = dot3(x_split, split(d), NT)
            parts.append(out * scale if g == 0 else out)
        parts.append(dot3(split(over_rows(yt_ref, b)), du_split, NN))
        whole = jnp.concatenate(parts, axis=0)
        for p in range(NP):
            big_ref[b, p] = whole[p * rows:(p + 1) * rows]

    def to_plane(src_of, dst, k):
        @pl.loop(1, NP)
        def _(s):
            p = lax.rem(plane_me + s, NP)
            copy_to(src_of(p), dst, k, plane_device(p)).start()

    def send_big(b):
        to_plane(lambda p: big_ref.at[b, p], bigr_ref.at[b, plane_me], 18 + 4 * b)
        bigr_ref[b, plane_me] = big_ref[b, plane_me]

    def total_of(ref, count):
        total = ref[0]
        for p in range(1, count):
            total = total + ref[p]
        return total

    def send_near(b):
        arrived(18 + 4 * b, bigr_ref.at[b, pl.ds(0, NP - 1)])
        msgs[b][0, 0:rows] = total_of(bigr_ref.at[b], NP)
        if b == 1:
            msgs[b][0, rows:rows + 8] = tiny_ref[b]

        @pl.loop(1, 4)
        def _(s):
            m = lax.rem(inner + s, 4)
            copy_to(msgs[b].at[0], nears[b].at[inner], 19 + 4 * b, z_device(block * 4 + m)).start()

        nears[b][inner] = msgs[b][0]

    def send_far(b):
        arrived(19 + 4 * b, nears[b].at[pl.ds(0, 3)])
        msgs[b][1] = total_of(nears[b], 4)

        @pl.loop(1, 4)
        def _(s):
            m = lax.rem(block + s, 4)
            copy_to(msgs[b].at[1], fars[b].at[block], 20 + 4 * b, z_device(m * 4 + inner)).start()

        fars[b][block] = msgs[b][1]

    def send_last(b):
        arrived(20 + 4 * b, fars[b].at[pl.ds(0, 3)])
        msgs[b][2] = total_of(fars[b], 4) * out_scale
        to_plane(lambda p: msgs[b].at[2], lasts[b].at[plane_me], 21 + 4 * b)
        lasts[b][plane_me] = msgs[b][2]

    def finish_big(b):
        arrived(21 + 4 * b, lasts[b].at[pl.ds(0, NP - 1)])
        for p in range(NP):
            first = p * rows
            while first < (p + 1) * rows:
                g, at = first // C, first % C
                count = min((p + 1) * rows - first, C - at)
                piece = lasts[b][p, first - p * rows:first - p * rows + count]
                if g < 4:
                    gproj_ref[b, g, at:at + count] = piece
                else:
                    gout_ref[b, at:at + count] = piece
                first += count

    def put_tiny(b, tiny):
        ggain_ref[b:b + 1] = tiny[0:1]
        gshift_ref[b:b + 1] = tiny[1:2]
        gbias_ref[b] = tiny[2:2 + HEADS]
        ggate_ref[b:b + 1] = tiny[6:7]
        gos_ref[b:b + 1] = tiny[7:8]

    def send_tiny_z():
        @pl.loop(1, Z)
        def _(s):
            copy_to(tiny_ref.at[0], tinyz_ref.at[z_at], 26, z_device(lax.rem(z_at + s, Z))).start()

        tinyz_ref[z_at] = tiny_ref[0]

    def send_tiny_plane():
        arrived(26, tinyz_ref.at[pl.ds(0, Z - 1)])
        tiny_ref[2] = total_of(tinyz_ref, Z)
        to_plane(lambda p: tiny_ref.at[2], tinyp_ref.at[plane_me], 27)
        tinyp_ref[plane_me] = tiny_ref[2]

    def finish_tiny():
        arrived(27, tinyp_ref.at[pl.ds(0, NP - 1)])
        put_tiny(0, total_of(tinyp_ref, NP) * out_scale)

    def gate_grad(b):
        total = None
        for i in range(R):
            d = dpt_ref[b, i, 3 * C:]
            total = d if total is None else total + d
        return jnp.sum(total.T, axis=0, keepdims=True)

    def bias_part(b, dbr, x_split):
        bw = jnp.concatenate([bw_ref[b], jnp.zeros((4, C), F32)], axis=0)
        d_split = split(dbr)
        dxt = dot3(split(bw.T), d_split, NN)
        dbw = dot3m(d_split, x_split, NT)
        return dxt, dbw[0:HEADS]

    def col_sum(x):
        return jnp.sum(x, axis=0, keepdims=True)

    n0, r0 = normalise(z_ref[0])
    n_ref[0] = n0
    r_ref[0] = r0
    x0_split = split((n0 * gain_ref[0:1] + shift_ref[0:1]).T)
    xt_ref[0, 0] = x0_split[0]
    xt_ref[0, 1] = x0_split[1]
    put_chunk(0, bias_rows(0, x0_split))
    pl.semaphore_wait(barrier, D - 1 + NP - 1)
    gather_z(0)
    prepare(0)
    forward_near(0)
    project(0, x0_split)
    forward_far(0)
    send_half(0, 0)
    prepare(1)
    gathered(0)
    for h in range(HEADS):
        bt_ref[0, h] = jnp.concatenate([gather_ref[0, :, i * HEADS + h, :] for i in range(R)], axis=0).T

    for m in range(2):
        attend(0, 2 * m, 2 * m + 2)
        part = slice(2 * m * N, (2 * m + 2) * N)
        z_ref[1, part] = z_ref[0, part] + update(0, 2 * m, 2 * m + 2)
        for row in range(8 * m, 8 * m + 8):
            put_stage(1, row, z_ref[1, row * D:(row + 1) * D])
        if m == 0:
            send_half(1, 0)
    nm, rm = normalise(z_ref[1])
    nm_ref[...] = nm
    rm_ref[...] = rm
    xm_split = split((nm * gain_ref[1:2] + shift_ref[1:2]).T)
    xt_ref[2, 0] = xm_split[0]
    xt_ref[2, 1] = xm_split[1]
    put_chunk(1, bias_rows(1, xm_split))
    gather_z(1)
    send_half(1, 1)
    forward_near(1)
    forward_far(1)
    send_half(0, 1)

    half_arrived(1, 0)
    half_arrived(1, 1)

    def columns_layout(x):
        return jnp.concatenate([get_recv(x, i * R + j) for j in range(R) for i in range(R)], axis=0)

    n1, r1 = normalise(columns_layout(1))
    n_ref[1] = n1
    r_ref[1] = r1
    x1_split = split((n1 * gain_ref[1:2] + shift_ref[1:2]).T)
    xt_ref[1, 0] = x1_split[0]
    xt_ref[1, 1] = x1_split[1]
    project(1, x1_split)
    gathered(1)
    for h in range(HEADS):
        bt_ref[1, h] = jnp.concatenate([gather_ref[1, :, i * HEADS + h, :] for i in range(R)], axis=0)

    def stage_back(slot, m, value):
        for row in range(8):
            put_stage(slot, 8 * m + row, value[row * D:(row + 1) * D])

    attend(1, 0, R)
    u1 = update(1, 0, R)
    stage_back(2, 0, u1[0:2 * N])
    stage_back(2, 1, u1[2 * N:])
    send_half(2, 0)

    half_arrived(0, 0)
    half_arrived(0, 1)
    du1 = columns_layout(0)

    def bias_grad_1():
        for h in range(HEADS):
            for i in range(R):
                put_stage(4, i * HEADS + h, db_ref[1, h, i * D:(i + 1) * D])
        reduce_y(0)

    du1_split = backward(1, du1, bias_grad_1)
    for m in range(2):
        part = slice(2 * m * N, (2 * m + 2) * N)
        dx = dx_local(1, 2 * m, 2 * m + 2).T
        dx_ref[part] = dx
        stage_back(3, m, normalise_back(dx * gain_ref[1:2], n_ref[1, part], r_ref[1, part]))
        send_half(3, m)
    reduce_z(0)
    big_grads(1, (xt_ref[1, 0], xt_ref[1, 1]), du1_split)
    send_big(1)
    tiny_ref[1, 0:1] = col_sum(dx_ref[...] * n_ref[1])
    tiny_ref[1, 1:2] = col_sum(dx_ref[...])
    tiny_ref[1, 6:7] = gate_grad(1)
    tiny_ref[1, 7:8] = col_sum(du1)
    dxm_t, dbw1 = bias_part(1, reduced(0), (xt_ref[2, 0], xt_ref[2, 1]))
    dxm = dxm_t.T
    tiny_ref[1, 0:1] += col_sum(dxm * nm_ref[...])
    tiny_ref[1, 1:2] += col_sum(dxm)
    tiny_ref[1, 2:2 + HEADS] = dbw1
    mg_ref[...] = up_ref[...] + normalise_back(dxm * gain_ref[1:2], nm_ref[...], rm_ref[...])
    send_near(1)
    half_arrived(3, 0)
    half_arrived(3, 1)
    send_half(2, 1)
    for i in range(R):
        for j in range(R):
            at = (i * R + j) * D
            mg_ref[at:at + D] += get_recv(3, j * R + i)

    def bias_grad_0():
        for h in range(HEADS):
            turned = db_ref[0, h].T
            for i in range(R):
                put_stage(5, i * HEADS + h, turned[i * D:(i + 1) * D])
        reduce_y(1)

    du0_split = backward(0, mg_ref[...], bias_grad_0)
    send_far(1)
    big_grads(0, (xt_ref[0, 0], xt_ref[0, 1]), du0_split)
    reduce_z(1)
    send_big(0)
    tiny_ref[0, 6:7] = gate_grad(0)
    tiny_ref[0, 7:8] = col_sum(mg_ref[...])
    dxt_ref[...] = dx_local(0, 0, R)
    half_arrived(2, 0)
    half_arrived(2, 1)
    for i in range(R):
        for j in range(R):
            at = (i * R + j) * D
            new_ref[pl.ds(i * N + j, D, stride=R)] = z_ref[1, at:at + D] + get_recv(2, j * R + i)
    send_last(1)
    send_near(0)
    dx0_t, dbw0 = bias_part(0, reduced(1), (xt_ref[0, 0], xt_ref[0, 1]))
    dx_ref[...] = (dxt_ref[...] + dx0_t).T
    tiny_ref[0, 0:1] = col_sum(dx_ref[...] * n_ref[0])
    tiny_ref[0, 1:2] = col_sum(dx_ref[...])
    tiny_ref[0, 2:2 + HEADS] = dbw0
    send_tiny_z()
    send_far(0)
    dz0 = normalise_back(dx_ref[...] * gain_ref[0:1], n_ref[0], r_ref[0])
    for i in range(R):
        for j in range(R):
            at = (i * R + j) * D
            igrad_ref[pl.ds(i * N + j, D, stride=R)] = mg_ref[at:at + D] + dz0[at:at + D]
    send_tiny_plane()
    finish_big(1)
    tiny1 = last1_ref[0, rows:rows + 8]
    for p in range(1, NP):
        tiny1 = tiny1 + last1_ref[p, rows:rows + 8]
    put_tiny(1, tiny1)
    send_last(0)
    finish_tiny()
    finish_big(0)

    for k, ref in sent:
        wait_bytes(ref, send_sem.at[k])


def copies(*refs):
    count = len(refs) // 2
    for k in range(count):
        refs[count + k][...] = refs[k][...]


def body(D, NC, pair, pair_grad, gain, shift, w, bw, gs, wo, os):
    R, N, C = pair.shape[1:]
    T = R * N
    NP = 2 * NC
    rows = 5 * C // NP
    vmem = pl.BlockSpec(memory_space=pltpu.VMEM)
    out = lambda *shape: jax.ShapeDtypeStruct(shape, F32)
    results = pl.pallas_call(
        functools.partial(kernel, D, NC),
        out_shape=[out(T, C), out(T, C), out(2, C), out(2, C), out(2, 4, C, C), out(2, HEADS, C), out(2, C),
                   out(2, C, C), out(2, C)],
        in_specs=[vmem] * 9,
        out_specs=[vmem] * 9,
        scratch_shapes=[
            pltpu.VMEM((2, T, C), F32),
            pltpu.VMEM((2, T, C), F32),
            pltpu.VMEM((2, T, 1), F32),
            pltpu.VMEM((T, C), F32),
            pltpu.VMEM((T, 1), F32),
            pltpu.VMEM((T, C), F32),
            pltpu.VMEM((T, C), F32),
            pltpu.VMEM((T, C), F32),
            pltpu.VMEM((C, T), F32),
            pltpu.VMEM((2, 2, 4 * C, C), BF16),
            pltpu.VMEM((3, 2, C, T), BF16),
            pltpu.VMEM((2, R, 4 * C, N), F32),
            pltpu.VMEM((2, R, HEADS, N, N), F32),
            pltpu.VMEM((2, R, C, N), F32),
            pltpu.VMEM((2, R, C, N), F32),
            pltpu.VMEM((R, C, N), F32),
            pltpu.VMEM((2, R, 4 * C, N), F32),
            pltpu.VMEM((2, HEADS, N, N), F32),
            pltpu.VMEM((2, HEADS, N, N), F32),
            pltpu.VMEM((6, D, R * R, C), F32),
            pltpu.VMEM((2, R * R, N), F32),
            pltpu.VMEM((4, D, R * R, C), F32),
            pltpu.VMEM((2, D, R * R, C), F32),
            pltpu.VMEM((2, Z, R * R, C), F32),
            pltpu.VMEM((2, Z, R * R, C), F32),
            pltpu.VMEM((2, Z, R * R, C), F32),
            pltpu.VMEM((2, NP, rows, C), F32),
            pltpu.VMEM((2, NP, rows, C), F32),
            pltpu.VMEM((3, rows, C), F32),
            pltpu.VMEM((3, rows + 8, C), F32),
            pltpu.VMEM((4, rows, C), F32),
            pltpu.VMEM((4, rows + 8, C), F32),
            pltpu.VMEM((4, rows, C), F32),
            pltpu.VMEM((4, rows + 8, C), F32),
            pltpu.VMEM((NP, rows, C), F32),
            pltpu.VMEM((NP, rows + 8, C), F32),
            pltpu.VMEM((3, 8, C), F32),
            pltpu.VMEM((Z, 8, C), F32),
            pltpu.VMEM((NP, 8, C), F32),
            pltpu.SemaphoreType.DMA((28,)),
            pltpu.SemaphoreType.DMA((28,)),
        ],
        compiler_params=pltpu.CompilerParams(
            collective_id=0, has_side_effects=True, vmem_limit_bytes=56 * 1024 * 1024),
    )(pair.reshape(T, C), pair_grad.reshape(T, C), gain, shift, w, bw, gs, wo, os)
    results = pl.pallas_call(
        copies,
        out_shape=[jax.ShapeDtypeStruct(r.shape, F32) for r in results],
        in_specs=[vmem] * 9,
        out_specs=[vmem] * 9,
        compiler_params=pltpu.CompilerParams(vmem_limit_bytes=16 * 1024 * 1024),
    )(*results)
    return (results[0].reshape(pair.shape), results[1].reshape(pair.shape)) + tuple(results[2:])


def solution(mesh):
    rows = P("crop", "dap", None, None)
    return jax.shard_map(
        functools.partial(body, mesh.shape["dap"], mesh.shape["crop"]),
        mesh=mesh,
        in_specs=(rows, rows) + (P(),) * 7,
        out_specs=(rows, rows) + (P(),) * 7,
        check_vma=False,
    )
```

```python
import functools

import jax
import jax.numpy as jnp
from jax import lax
from jax.experimental import pallas as pl
from jax.experimental.pallas import tpu as pltpu
from jax.sharding import PartitionSpec as P

HEADS = 4
EPSILON = 1e-05
F32 = jnp.float32
BF16 = jnp.bfloat16
MESH = pl.DeviceIdType.MESH
NN = (((1,), (0,)), ((), ()))
NT = (((1,), (1,)), ((), ()))
Z = 16


def split(x):
    hi = x.astype(BF16)
    return hi, (x - hi.astype(F32)).astype(BF16)


def dot(a, b, dims):
    return lax.dot_general(a, b, dims, preferred_element_type=F32)


def dot3(a, b, dims):
    return dot(a[0], b[0], dims) + (dot(a[0], b[1], dims) + dot(a[1], b[0], dims))


def dot3m(a, b, dims):
    rows = a[0].shape[0]
    both = dot(jnp.concatenate(a, axis=0), b[0], dims)
    return both[:rows] + (both[rows:] + dot(a[0], b[1], dims))


def dot_tn(a, b):
    ah, al = split(a)
    bh, bl = split(b)
    stacked = jnp.concatenate([ah.astype(F32), ah.astype(F32), al.astype(F32), al.astype(F32)], axis=0)
    return dot(stacked.T.astype(BF16), jnp.concatenate([bh, bl, bh, bl], axis=0), NN)


def normalise(z):
    center = z - jnp.mean(z, axis=-1, keepdims=True)
    spread = jnp.mean(center * center, axis=-1, keepdims=True)
    r = lax.rsqrt(spread + EPSILON)
    return center * r, r


def normalise_back(dn, n, r):
    first = jnp.mean(dn, axis=-1, keepdims=True)
    second = jnp.mean(dn * n, axis=-1, keepdims=True)
    return r * (dn - first - n * second)


def kernel(
    D,
    NC,
    *refs,
):
    given, results, held, filled, refs = refs[:9], refs[9:18], refs[18:27], refs[27:36], refs[36:]
    body_of(D, NC, given, results, held, filled, *refs)


def body_of(
    D,
    NC,
    given, results, held, filled,
    in_sem, out_sem,
    z_ref, n_ref, r_ref, nm_ref, rm_ref, up_ref, mg_ref, dx_ref, dxt_ref,
    wt_ref, xt_ref, pt_ref, at_ref, ot_ref, yt_ref, dot_ref, dpt_ref, bt_ref, db_ref,
    stage_ref, chunk_ref, recv_ref, gather_ref, pairsum_ref, zstage_ref, zrecv_ref, direct_ref,
    big_ref, bigr_ref, msg0_ref, msg1_ref, near0_ref, near1_ref, far0_ref, far1_ref, last0_ref, last1_ref,
    tiny_ref, tinyz_ref, tinyp_ref,
    send_sem, recv_sem,
):
    pair_ref, grad_ref, gain_ref, shift_ref, w_ref, bw_ref, gs_ref, wo_ref, os_ref = held
    new_ref, igrad_ref, ggain_ref, gshift_ref, gproj_ref, gbias_ref, ggate_ref, gout_ref, gos_ref = filled
    R = 4
    N = R * D
    T = R * N
    C = 128
    HS = C // HEADS
    scale = HS ** (-0.5)
    out_scale = 1.0 / (NC * N)
    me = lax.axis_index("dap")
    crop = lax.axis_index("crop")
    y_at, z_at = me // Z, lax.rem(me, Z)
    block, inner = z_at // 4, lax.rem(z_at, 4)
    NP = 2 * NC
    plane_me = crop * 2 + y_at
    rows = 5 * C // NP

    barrier = pltpu.get_barrier_semaphore()

    def plane_device(p):
        return (p // 2, lax.rem(p, 2) * Z + z_at)

    def z_device(z):
        return (crop, y_at * Z + z)

    partner = (crop, (1 - y_at) * Z + z_at)

    def greet(y, z):
        device = (crop, lax.rem(y, 2) * Z + lax.rem(z, Z))
        pl.semaphore_signal(barrier, inc=1, device_id=device, device_id_type=MESH)

    greet(y_at, z_at + 8)
    greet(y_at + 1, z_at + 8)

    @pl.loop(1, 8)
    def _(s):
        greet(y_at, z_at + 8 - s)
        greet(y_at, z_at + 8 + s)
        greet(y_at + 1, z_at + 8 - s)
        greet(y_at + 1, z_at + 8 + s)

    greet(y_at + 1, z_at)

    @pl.loop(1, NP)
    def _(s):
        pl.semaphore_signal(barrier, inc=1, device_id=plane_device(lax.rem(plane_me + s, NP)), device_id_type=MESH)

    fetches = [pltpu.make_async_copy(given[k], held[k], in_sem.at[k]) for k in range(9)]
    stores = [pltpu.make_async_copy(filled[k], results[k], out_sem.at[k]) for k in range(9)]
    for k in (0, 2, 3, 5, 4, 6, 1, 7, 8):
        fetches[k].start()

    def copy_to(src, dst, k, device):
        return pltpu.make_async_remote_copy(
            src_ref=src, dst_ref=dst, send_sem=send_sem.at[k], recv_sem=recv_sem.at[k],
            device_id=device, device_id_type=MESH)

    def wait_bytes(ref, sem):
        pltpu.make_async_copy(ref, ref, sem).wait()

    sent = []

    def arrived(k, ref):
        wait_bytes(ref, recv_sem.at[k])
        sent.append((k, ref))

    def send_half(x, m):
        k = 2 * x + m
        part = pl.ds(8 * m, 8)

        def to(y, z):
            peer = lax.rem(y, 2) * Z + lax.rem(z, Z)
            copy_to(stage_ref.at[x, peer, part], recv_ref.at[x, me, part], k, (crop, peer)).start()

        to(y_at, z_at + 8)
        to(y_at + 1, z_at + 8)

        @pl.loop(1, 8)
        def _(s):
            to(y_at, z_at + 8 - s)
            to(y_at, z_at + 8 + s)
            to(y_at + 1, z_at + 8 - s)
            to(y_at + 1, z_at + 8 + s)

        to(y_at + 1, z_at)
        recv_ref[x, me, part] = stage_ref[x, me, part]

    def half_arrived(x, m):
        arrived(2 * x + m, recv_ref.at[x, pl.ds(0, D - 1), pl.ds(8 * m, 8)])

    def near_z(s):
        return lax.rem(z_at + 12 + s + s // 4, Z)

    def middle_z(s):
        return lax.rem(z_at + 5 + s + 3 * (s // 2), Z)

    def far_z(s):
        return lax.rem(z_at + 7 + s, Z)

    def gather_z(g):
        def to(y, z, k):
            copy_to(chunk_ref.at[g], gather_ref.at[g, me], k, (crop, y * Z + z)).start()

        @pl.loop(0, 3)
        def _(s):
            to(y_at, far_z(s), 10 + 4 * g)
            if g == 0:
                to(1 - y_at, far_z(s), 10 + 4 * g)

        @pl.loop(0, 4)
        def _(s):
            to(y_at, middle_z(s), 9 + 4 * g)

        @pl.loop(0, 8)
        def _(s):
            to(y_at, near_z(s), 8 + 4 * g)

        gather_ref[g, me] = chunk_ref[g]

    def forward(g):
        def to(z):
            slot = y_at * Z + z
            copy_to(gather_ref.at[g, slot], gather_ref.at[g, slot], 11 + 4 * g, partner).start()

        to(z_at)
        arrived(8 + 4 * g, gather_ref.at[g, pl.ds(0, 8)])

        @pl.loop(0, 8)
        def _(s):
            to(near_z(s))

        arrived(9 + 4 * g, gather_ref.at[g, pl.ds(0, 4)])

        @pl.loop(0, 4)
        def _(s):
            to(middle_z(s))

        if g == 1:
            arrived(10 + 4 * g, gather_ref.at[g, pl.ds(0, 3)])

            @pl.loop(0, 3)
            def _(s):
                to(far_z(s))

    def gathered(g):
        if g == 0:
            arrived(10, gather_ref.at[g, pl.ds(0, 6)])
        arrived(11 + 4 * g, gather_ref.at[g, pl.ds(0, 13 + 3 * g)])

    def reduce_y():
        copy_to(stage_ref.at[4, pl.ds((1 - y_at) * Z, Z)], pairsum_ref.at[0], 16, partner).start()

    def reduce_z():
        arrived(16, pairsum_ref.at[0])
        zstage_ref[0] = stage_ref[4, pl.ds(y_at * Z, Z)] + pairsum_ref[0]

        @pl.loop(1, Z)
        def _(s):
            z = lax.rem(z_at + s, Z)
            copy_to(zstage_ref.at[0, z], zrecv_ref.at[0, z_at], 17, z_device(z)).start()

        zrecv_ref[0, z_at] = zstage_ref[0, z_at]

    def swift_y():
        @pl.loop(0, 5)
        def _(s):
            z = lax.rem(z_at + 6 + s, Z)
            copy_to(stage_ref.at[5, y_at * Z + z], direct_ref.at[s], 28, (crop, y_at * Z + z)).start()
            other = (1 - y_at) * Z + z
            copy_to(stage_ref.at[5, other], direct_ref.at[5 + s], 28, (crop, other)).start()

        @pl.loop(0, 11)
        def _(s):
            z = lax.rem(z_at + 11 + s, Z)
            copy_to(stage_ref.at[5, (1 - y_at) * Z + z], pairsum_ref.at[1, s], 18, partner).start()

    def swift_z():
        arrived(18, pairsum_ref.at[1, pl.ds(0, 11)])

        @pl.loop(0, 11)
        def _(s):
            z = lax.rem(z_at + 11 + s, Z)
            zstage_ref[1, s] = stage_ref[5, y_at * Z + z] + pairsum_ref[1, s]

        @pl.loop(0, 5)
        def _(s):
            for at in (s, 10 - s):
                copy_to(zstage_ref.at[1, at], zrecv_ref.at[1, at], 19, z_device(lax.rem(z_at + 11 + at, Z))).start()

        zrecv_ref[1, 5] = zstage_ref[1, 5]

    def token_rows(total):
        whole = jnp.concatenate([total[i * HEADS:(i + 1) * HEADS] for i in range(R)], axis=1)
        return jnp.concatenate([whole, jnp.zeros((4, T), F32)], axis=0)

    def reduced():
        arrived(17, zrecv_ref.at[0, pl.ds(0, Z - 1)])
        return token_rows(total_of(zrecv_ref.at[0], Z))

    def swift_reduced():
        arrived(28, direct_ref)
        arrived(19, zrecv_ref.at[1, pl.ds(0, 10)])
        return token_rows(total_of(zrecv_ref.at[1], 11) + total_of(direct_ref, 10))

    def put_stage(slot, row, tile):
        stage_ref[slot, :, row, :] = tile

    def get_recv(x, row):
        return recv_ref[x, :, row, :]

    def prepare(b):
        for g in range(4):
            w = w_ref[b, g]
            if g == 0:
                w = w * scale
            hi, lo = split(w.T)
            wt_ref[b, 0, g * C:(g + 1) * C] = hi
            wt_ref[b, 1, g * C:(g + 1) * C] = lo

    def columns(b):
        rows = jnp.concatenate([gs_ref[b:b + 1], jnp.zeros((7, C), F32)], axis=0)
        return rows.T[:, 0:1]

    def bias_rows(b, x_split):
        bw = jnp.concatenate([bw_ref[b], jnp.zeros((4, C), F32)], axis=0)
        return dot3m(split(bw), x_split, NN)

    def put_chunk(slot, rows):
        for i in range(R):
            chunk_ref[slot, i * HEADS:(i + 1) * HEADS] = rows[0:HEADS, i * N:(i + 1) * N]

    def project(b, x_split):
        out = dot3((wt_ref[b, 0], wt_ref[b, 1]), x_split, NN)
        out_gate = jax.nn.sigmoid(out[3 * C:] + columns(b))
        for i in range(R):
            pt_ref[b, i, 0:3 * C] = out[0:3 * C, i * N:(i + 1) * N]
            pt_ref[b, i, 3 * C:] = out_gate[:, i * N:(i + 1) * N]

    def attend(b, lo, hi):
        for i in range(lo, hi):
            for h in range(HEADS):
                at = h * HS
                q = pt_ref[b, i, at:at + HS]
                k = pt_ref[b, i, C + at:C + at + HS]
                v = pt_ref[b, i, 2 * C + at:2 * C + at + HS]
                s = dot_tn(k, q) + bt_ref[b, h]
                e = jnp.exp(s - jnp.max(s, axis=0, keepdims=True))
                a = e * (1.0 / jnp.sum(e, axis=0, keepdims=True))
                at_ref[b, i, h] = a
                o = dot3m(split(v), split(a), NN)
                ot_ref[b, i, at:at + HS] = o
                yt_ref[b, i, at:at + HS] = o * pt_ref[b, i, 3 * C + at:3 * C + at + HS]

    def over_rows(ref, b, lo=0, hi=R):
        return jnp.concatenate([ref[b, i] for i in range(lo, hi)], axis=1)

    def update(b, lo, hi):
        ut = dot3(split(wo_ref[b].T), split(over_rows(yt_ref, b, lo, hi)), NN)
        return ut.T + os_ref[b:b + 1]

    def backward(b, du_split, lo, hi):
        dyt = dot3(split(wo_ref[b]), du_split, NT)
        for i in range(lo, hi):
            dy = dyt[:, (i - lo) * N:(i - lo + 1) * N]
            gate = pt_ref[b, i, 3 * C:]
            dot_ref[i] = dy * gate
            dpt_ref[b, i, 3 * C:] = dy * ot_ref[b, i] * (gate * (1.0 - gate))
        for i in range(lo, hi):
            for h in range(HEADS):
                at = h * HS
                q = pt_ref[b, i, at:at + HS]
                k = pt_ref[b, i, C + at:C + at + HS]
                v = pt_ref[b, i, 2 * C + at:2 * C + at + HS]
                a = at_ref[b, i, h]
                do = dot_ref[i, at:at + HS]
                row = jnp.sum(do * ot_ref[b, i, at:at + HS], axis=0, keepdims=True)
                ds = a * (dot_tn(v, do) - row)
                if i == 0:
                    db_ref[b, h] = ds
                else:
                    db_ref[b, h] += ds
                ds_split = split(ds)
                dpt_ref[b, i, at:at + HS] = dot3m(split(k), ds_split, NN)
                dpt_ref[b, i, C + at:C + at + HS] = dot3m(split(q), ds_split, NT)
                dpt_ref[b, i, 2 * C + at:2 * C + at + HS] = dot3m(split(do), split(a), NT)

    def dx_local(b, lo, hi):
        total = None
        for g in range(4):
            w = w_ref[b, g]
            if g == 0:
                w = w * scale
            d = jnp.concatenate([dpt_ref[b, i, g * C:(g + 1) * C] for i in range(lo, hi)], axis=1)
            term = dot3(split(w), split(d), NN)
            total = term if total is None else total + term
        return total

    msgs, nears, fars, lasts = (msg0_ref, msg1_ref), (near0_ref, near1_ref), (far0_ref, far1_ref), (last0_ref, last1_ref)

    def big_grads(b, x_split, du_split):
        parts = []
        for g in range(4):
            d = jnp.concatenate([dpt_ref[b, i, g * C:(g + 1) * C] for i in range(R)], axis=1)
            out = dot3(x_split, split(d), NT)
            parts.append(out * scale if g == 0 else out)
        parts.append(dot3(split(over_rows(yt_ref, b)), du_split, NN))
        whole = jnp.concatenate(parts, axis=0)
        for p in range(NP):
            big_ref[b, p] = whole[p * rows:(p + 1) * rows]

    def to_plane(src_of, dst, k):
        def to(s):
            p = lax.rem(plane_me + s, NP)
            copy_to(src_of(p), dst, k, plane_device(p)).start()

        to(NC)

        @pl.loop(1, NC)
        def _(s):
            to(NC - s)
            to(NC + s)

    def send_big(b):
        to_plane(lambda p: big_ref.at[b, p], bigr_ref.at[b, plane_me], 20 + 4 * b)
        bigr_ref[b, plane_me] = big_ref[b, plane_me]

    def total_of(ref, count):
        total = ref[0]
        for p in range(1, count):
            total = total + ref[p]
        return total

    def send_near(b):
        arrived(20 + 4 * b, bigr_ref.at[b, pl.ds(0, NP - 1)])
        msgs[b][0, 0:rows] = total_of(bigr_ref.at[b], NP)
        if b == 1:
            msgs[b][0, rows:rows + 8] = tiny_ref[b]

        @pl.loop(1, 4)
        def _(s):
            m = lax.rem(inner + s, 4)
            copy_to(msgs[b].at[0], nears[b].at[inner], 21 + 4 * b, z_device(block * 4 + m)).start()

        nears[b][inner] = msgs[b][0]

    def send_far(b):
        arrived(21 + 4 * b, nears[b].at[pl.ds(0, 3)])
        msgs[b][1] = total_of(nears[b], 4)

        @pl.loop(1, 4)
        def _(s):
            m = lax.rem(block + s, 4)
            copy_to(msgs[b].at[1], fars[b].at[block], 22 + 4 * b, z_device(m * 4 + inner)).start()

        fars[b][block] = msgs[b][1]

    def send_last(b):
        arrived(22 + 4 * b, fars[b].at[pl.ds(0, 3)])
        msgs[b][2] = total_of(fars[b], 4) * out_scale
        to_plane(lambda p: msgs[b].at[2], lasts[b].at[plane_me], 23 + 4 * b)
        lasts[b][plane_me] = msgs[b][2]

    def finish_big(b):
        arrived(23 + 4 * b, lasts[b].at[pl.ds(0, NP - 1)])
        for p in range(NP):
            first = p * rows
            while first < (p + 1) * rows:
                g, at = first // C, first % C
                count = min((p + 1) * rows - first, C - at)
                piece = lasts[b][p, first - p * rows:first - p * rows + count]
                if g < 4:
                    gproj_ref[b, g, at:at + count] = piece
                else:
                    gout_ref[b, at:at + count] = piece
                first += count

    def put_tiny(b, tiny):
        ggain_ref[b:b + 1] = tiny[0:1]
        gshift_ref[b:b + 1] = tiny[1:2]
        gbias_ref[b] = tiny[2:2 + HEADS]
        ggate_ref[b:b + 1] = tiny[6:7]
        gos_ref[b:b + 1] = tiny[7:8]

    def send_tiny_z():
        @pl.loop(1, Z)
        def _(s):
            copy_to(tiny_ref.at[0], tinyz_ref.at[z_at], 29, z_device(lax.rem(z_at + s, Z))).start()

        tinyz_ref[z_at] = tiny_ref[0]

    def send_tiny_plane():
        arrived(29, tinyz_ref.at[pl.ds(0, Z - 1)])
        tiny_ref[2] = total_of(tinyz_ref, Z)
        to_plane(lambda p: tiny_ref.at[2], tinyp_ref.at[plane_me], 30)
        tinyp_ref[plane_me] = tiny_ref[2]

    def finish_tiny():
        arrived(30, tinyp_ref.at[pl.ds(0, NP - 1)])
        put_tiny(0, total_of(tinyp_ref, NP) * out_scale)

    def gate_grad(b):
        total = None
        for i in range(R):
            d = dpt_ref[b, i, 3 * C:]
            total = d if total is None else total + d
        return jnp.sum(total.T, axis=0, keepdims=True)

    def bias_part(b, dbr, x_split):
        bw = jnp.concatenate([bw_ref[b], jnp.zeros((4, C), F32)], axis=0)
        d_split = split(dbr)
        dxt = dot3(split(bw.T), d_split, NN)
        dbw = dot3m(d_split, x_split, NT)
        return dxt, dbw[0:HEADS]

    def col_sum(x):
        return jnp.sum(x, axis=0, keepdims=True)

    fetches[0].wait()
    for i in range(R):
        for j in range(R):
            at = (i * R + j) * D
            z_ref[0, at:at + D] = pair_ref[pl.ds(i * N + j, D, stride=R)]
    fetches[2].wait()
    fetches[3].wait()
    fetches[5].wait()
    n0, r0 = normalise(z_ref[0])
    n_ref[0] = n0
    r_ref[0] = r0
    x0_split = split((n0 * gain_ref[0:1] + shift_ref[0:1]).T)
    xt_ref[0, 0] = x0_split[0]
    xt_ref[0, 1] = x0_split[1]
    put_chunk(0, bias_rows(0, x0_split))
    fetches[4].wait()
    fetches[6].wait()
    prepare(0)
    pl.semaphore_wait(barrier, D - 1 + NP - 1)
    gather_z(0)
    fetches[1].wait()
    for i in range(R):
        for j in range(R):
            at = (i * R + j) * D
            tile = grad_ref[pl.ds(i * N + j, D, stride=R)]
            up_ref[at:at + D] = tile
            put_stage(0, j * R + i, tile)
    project(0, x0_split)
    forward(0)
    send_half(0, 0)
    prepare(1)
    fetches[7].wait()
    fetches[8].wait()
    gathered(0)
    for h in range(HEADS):
        bt_ref[0, h] = jnp.concatenate([gather_ref[0, :, i * HEADS + h, :] for i in range(R)], axis=0).T

    for m in range(2):
        attend(0, 2 * m, 2 * m + 2)
        part = slice(2 * m * N, (2 * m + 2) * N)
        z_ref[1, part] = z_ref[0, part] + update(0, 2 * m, 2 * m + 2)
        for row in range(8 * m, 8 * m + 8):
            put_stage(1, row, z_ref[1, row * D:(row + 1) * D])
        if m == 0:
            send_half(1, 0)
    nm, rm = normalise(z_ref[1])
    nm_ref[...] = nm
    rm_ref[...] = rm
    xm_split = split((nm * gain_ref[1:2] + shift_ref[1:2]).T)
    xt_ref[2, 0] = xm_split[0]
    xt_ref[2, 1] = xm_split[1]
    put_chunk(1, bias_rows(1, xm_split))
    gather_z(1)
    send_half(1, 1)
    forward(1)

    half_arrived(1, 0)
    send_half(0, 1)
    half_arrived(1, 1)
    n1, r1 = normalise(
        jnp.concatenate([get_recv(1, i * R + j) for j in range(R) for i in range(R)], axis=0))
    n_ref[1] = n1
    r_ref[1] = r1
    x1_split = split((n1 * gain_ref[1:2] + shift_ref[1:2]).T)
    xt_ref[1, 0] = x1_split[0]
    xt_ref[1, 1] = x1_split[1]
    project(1, x1_split)
    gathered(1)
    for h in range(HEADS):
        bt_ref[1, h] = jnp.concatenate([gather_ref[1, :, i * HEADS + h, :] for i in range(R)], axis=0)

    def stage_back(slot, m, value):
        for row in range(8):
            put_stage(slot, 8 * m + row, value[row * D:(row + 1) * D])

    for m in range(2):
        attend(1, 2 * m, 2 * m + 2)
        stage_back(2, m, update(1, 2 * m, 2 * m + 2))

    du1_halves = []
    for m in range(2):
        part = slice(2 * m * N, (2 * m + 2) * N)
        half_arrived(0, m)
        du1_halves.append(jnp.concatenate([get_recv(0, 8 * m + row) for row in range(8)], axis=0))
        backward(1, split(du1_halves[m]), 2 * m, 2 * m + 2)
        if m == 1:
            for h in range(HEADS):
                for i in range(R):
                    put_stage(4, i * HEADS + h, db_ref[1, h, i * D:(i + 1) * D])
            reduce_y()
        dx = dx_local(1, 2 * m, 2 * m + 2).T
        dx_ref[part] = dx
        stage_back(3, m, normalise_back(dx * gain_ref[1:2], n_ref[1, part], r_ref[1, part]))
        send_half(3, m)
    reduce_z()
    du1 = jnp.concatenate(du1_halves, axis=0)
    big_grads(1, (xt_ref[1, 0], xt_ref[1, 1]), split(du1))
    send_big(1)
    tiny_ref[1, 0:1] = col_sum(dx_ref[...] * n_ref[1])
    tiny_ref[1, 1:2] = col_sum(dx_ref[...])
    tiny_ref[1, 6:7] = gate_grad(1)
    tiny_ref[1, 7:8] = col_sum(du1)
    dxm_t, dbw1 = bias_part(1, reduced(), (xt_ref[2, 0], xt_ref[2, 1]))
    dxm = dxm_t.T
    tiny_ref[1, 0:1] += col_sum(dxm * nm_ref[...])
    tiny_ref[1, 1:2] += col_sum(dxm)
    tiny_ref[1, 2:2 + HEADS] = dbw1
    mg_ref[...] = up_ref[...] + normalise_back(dxm * gain_ref[1:2], nm_ref[...], rm_ref[...])
    send_near(1)
    half_arrived(3, 0)
    half_arrived(3, 1)
    send_half(2, 0)
    for i in range(R):
        for j in range(R):
            at = (i * R + j) * D
            mg_ref[at:at + D] += get_recv(3, j * R + i)

    du0_split = split(mg_ref[...])
    backward(0, du0_split, 0, R)
    for h in range(HEADS):
        turned = db_ref[0, h].T
        for i in range(R):
            put_stage(5, i * HEADS + h, turned[i * D:(i + 1) * D])
    swift_y()
    send_far(1)
    big_grads(0, (xt_ref[0, 0], xt_ref[0, 1]), du0_split)
    swift_z()
    send_big(0)
    tiny_ref[0, 6:7] = gate_grad(0)
    tiny_ref[0, 7:8] = col_sum(mg_ref[...])
    dxt_ref[...] = dx_local(0, 0, R)
    send_last(1)
    send_near(0)
    dx0_t, dbw0 = bias_part(0, swift_reduced(), (xt_ref[0, 0], xt_ref[0, 1]))
    dx_ref[...] = (dxt_ref[...] + dx0_t).T
    tiny_ref[0, 0:1] = col_sum(dx_ref[...] * n_ref[0])
    tiny_ref[0, 1:2] = col_sum(dx_ref[...])
    tiny_ref[0, 2:2 + HEADS] = dbw0
    send_tiny_z()
    send_half(2, 1)
    send_far(0)
    dz0 = normalise_back(dx_ref[...] * gain_ref[0:1], n_ref[0], r_ref[0])
    for i in range(R):
        for j in range(R):
            at = (i * R + j) * D
            igrad_ref[pl.ds(i * N + j, D, stride=R)] = mg_ref[at:at + D] + dz0[at:at + D]
    stores[1].start()
    send_tiny_plane()
    for j in range(R):
        if j % 2 == 0:
            half_arrived(2, j // 2)
        for i in range(R):
            at = (i * R + j) * D
            new_ref[pl.ds(i * N + j, D, stride=R)] = z_ref[1, at:at + D] + get_recv(2, j * R + i)
    stores[0].start()
    finish_big(1)
    tiny1 = last1_ref[0, rows:rows + 8]
    for p in range(1, NP):
        tiny1 = tiny1 + last1_ref[p, rows:rows + 8]
    put_tiny(1, tiny1)
    send_last(0)
    finish_tiny()
    finish_big(0)

    for k in range(2, 9):
        stores[k].start()

    for k, ref in sent:
        wait_bytes(ref, send_sem.at[k])
    for store in stores:
        store.wait()


def copies(*refs):
    ins, outs, held, sems = refs[:9], refs[9:18], refs[18:27], refs[27]
    fetches = [pltpu.make_async_copy(ins[k], held[k], sems.at[0, k]) for k in range(9)]
    stores = [pltpu.make_async_copy(held[k], outs[k], sems.at[1, k]) for k in range(9)]
    for fetch in fetches:
        fetch.start()
    for fetch, store in zip(fetches, stores):
        fetch.wait()
        store.start()
    for store in stores:
        store.wait()


def body(D, NC, pair, pair_grad, gain, shift, w, bw, gs, wo, os):
    R, N, C = pair.shape[1:]
    T = R * N
    NP = 2 * NC
    rows = 5 * C // NP
    anywhere = pl.BlockSpec(memory_space=pl.ANY)
    out = lambda *shape: jax.ShapeDtypeStruct(shape, F32)
    args = (pair.reshape(T, C), pair_grad.reshape(T, C), gain, shift, w, bw, gs, wo, os)
    shapes_in = [out(*a.shape) for a in args]
    shapes_out = [out(T, C), out(T, C), out(2, C), out(2, C), out(2, 4, C, C), out(2, HEADS, C), out(2, C),
                  out(2, C, C), out(2, C)]
    results = pl.pallas_call(
        functools.partial(kernel, D, NC),
        out_shape=shapes_out,
        in_specs=[anywhere] * 9,
        out_specs=[anywhere] * 9,
        scratch_shapes=[pltpu.VMEM(s.shape, F32) for s in shapes_in + shapes_out] + [
            pltpu.SemaphoreType.DMA((9,)),
            pltpu.SemaphoreType.DMA((9,)),
            pltpu.VMEM((2, T, C), F32),
            pltpu.VMEM((2, T, C), F32),
            pltpu.VMEM((2, T, 1), F32),
            pltpu.VMEM((T, C), F32),
            pltpu.VMEM((T, 1), F32),
            pltpu.VMEM((T, C), F32),
            pltpu.VMEM((T, C), F32),
            pltpu.VMEM((T, C), F32),
            pltpu.VMEM((C, T), F32),
            pltpu.VMEM((2, 2, 4 * C, C), BF16),
            pltpu.VMEM((3, 2, C, T), BF16),
            pltpu.VMEM((2, R, 4 * C, N), F32),
            pltpu.VMEM((2, R, HEADS, N, N), F32),
            pltpu.VMEM((2, R, C, N), F32),
            pltpu.VMEM((2, R, C, N), F32),
            pltpu.VMEM((R, C, N), F32),
            pltpu.VMEM((2, R, 4 * C, N), F32),
            pltpu.VMEM((2, HEADS, N, N), F32),
            pltpu.VMEM((2, HEADS, N, N), F32),
            pltpu.VMEM((6, D, R * R, C), F32),
            pltpu.VMEM((2, R * R, N), F32),
            pltpu.VMEM((4, D, R * R, C), F32),
            pltpu.VMEM((2, D, R * R, C), F32),
            pltpu.VMEM((2, Z, R * R, C), F32),
            pltpu.VMEM((2, Z, R * R, C), F32),
            pltpu.VMEM((2, Z, R * R, C), F32),
            pltpu.VMEM((10, R * R, C), F32),
            pltpu.VMEM((2, NP, rows, C), F32),
            pltpu.VMEM((2, NP, rows, C), F32),
            pltpu.VMEM((3, rows, C), F32),
            pltpu.VMEM((3, rows + 8, C), F32),
            pltpu.VMEM((4, rows, C), F32),
            pltpu.VMEM((4, rows + 8, C), F32),
            pltpu.VMEM((4, rows, C), F32),
            pltpu.VMEM((4, rows + 8, C), F32),
            pltpu.VMEM((NP, rows, C), F32),
            pltpu.VMEM((NP, rows + 8, C), F32),
            pltpu.VMEM((3, 8, C), F32),
            pltpu.VMEM((Z, 8, C), F32),
            pltpu.VMEM((NP, 8, C), F32),
            pltpu.SemaphoreType.DMA((31,)),
            pltpu.SemaphoreType.DMA((31,)),
        ],
        compiler_params=pltpu.CompilerParams(
            collective_id=0, has_side_effects=True, vmem_limit_bytes=56 * 1024 * 1024),
    )(*args)
    results = pl.pallas_call(
        copies,
        out_shape=shapes_out,
        in_specs=[anywhere] * 9,
        out_specs=[anywhere] * 9,
        scratch_shapes=[pltpu.VMEM(s.shape, F32) for s in shapes_out] + [pltpu.SemaphoreType.DMA((2, 9))],
        compiler_params=pltpu.CompilerParams(vmem_limit_bytes=56 * 1024 * 1024),
    )(*results)
    return (results[0].reshape(pair.shape), results[1].reshape(pair.shape)) + tuple(results[2:])


def solution(mesh):
    rows = P("crop", "dap", None, None)
    return jax.shard_map(
        functools.partial(body, mesh.shape["dap"], mesh.shape["crop"]),
        mesh=mesh,
        in_specs=(rows, rows) + (P(),) * 7,
        out_specs=(rows, rows) + (P(),) * 7,
        check_vma=False,
    )
```

```python
import functools

import jax
import jax.numpy as jnp
from jax import lax
from jax.experimental import pallas as pl
from jax.experimental.pallas import tpu as pltpu
from jax.sharding import PartitionSpec as P

HEADS = 4
EPSILON = 1e-05
F32 = jnp.float32
BF16 = jnp.bfloat16
MESH = pl.DeviceIdType.MESH
NN = (((1,), (0,)), ((), ()))
NT = (((1,), (1,)), ((), ()))
Z = 16


def split(x):
    hi = x.astype(BF16)
    return hi, (x - hi.astype(F32)).astype(BF16)


def dot(a, b, dims):
    return lax.dot_general(a, b, dims, preferred_element_type=F32)


def dot3(a, b, dims):
    return dot(a[0], b[0], dims) + (dot(a[0], b[1], dims) + dot(a[1], b[0], dims))


def dot3m(a, b, dims):
    rows = a[0].shape[0]
    both = dot(jnp.concatenate(a, axis=0), b[0], dims)
    return both[:rows] + (both[rows:] + dot(a[0], b[1], dims))


def dot_tn(a, b):
    ah, al = split(a)
    bh, bl = split(b)
    stacked = jnp.concatenate([ah.astype(F32), ah.astype(F32), al.astype(F32), al.astype(F32)], axis=0)
    return dot(stacked.T.astype(BF16), jnp.concatenate([bh, bl, bh, bl], axis=0), NN)


def normalise(z):
    center = z - jnp.mean(z, axis=-1, keepdims=True)
    spread = jnp.mean(center * center, axis=-1, keepdims=True)
    r = lax.rsqrt(spread + EPSILON)
    return center * r, r


def normalise_back(dn, n, r):
    first = jnp.mean(dn, axis=-1, keepdims=True)
    second = jnp.mean(dn * n, axis=-1, keepdims=True)
    return r * (dn - first - n * second)


def kernel(
    D,
    NC,
    *refs,
):
    given, results, held, filled, refs = refs[:9], refs[9:18], refs[18:27], refs[27:36], refs[36:]
    body_of(D, NC, given, results, held, filled, *refs)


def body_of(
    D,
    NC,
    given, results, held, filled,
    in_sem, out_sem,
    z_ref, n_ref, r_ref, nm_ref, rm_ref, up_ref, mg_ref, dx_ref, dxt_ref,
    wt_ref, xt_ref, pt_ref, at_ref, ot_ref, yt_ref, dot_ref, dpt_ref, bt_ref, db_ref,
    stage_ref, chunk_ref, recv_ref, gather_ref, pairsum_ref, zstage_ref, zrecv_ref, direct_ref,
    big_ref, bigr_ref, msg0_ref, msg1_ref, near0_ref, near1_ref, far0_ref, far1_ref, last0_ref, last1_ref,
    tiny_ref, tinyz_ref, tinyp_ref, column_ref,
    send_sem, recv_sem,
):
    pair_ref, grad_ref, gain_ref, shift_ref, w_ref, bw_ref, gs_ref, wo_ref, os_ref = held
    new_ref, igrad_ref, ggain_ref, gshift_ref, gproj_ref, gbias_ref, ggate_ref, gout_ref, gos_ref = filled
    R = 4
    N = R * D
    T = R * N
    C = 128
    HS = C // HEADS
    scale = HS ** (-0.5)
    out_scale = 1.0 / (NC * N)
    me = lax.axis_index("dap")
    crop = lax.axis_index("crop")
    y_at, z_at = me // Z, lax.rem(me, Z)
    block, inner = z_at // 4, lax.rem(z_at, 4)
    NP = 2 * NC
    plane_me = crop * 2 + y_at
    rows = 5 * C // NP

    barrier = pltpu.get_barrier_semaphore()

    def plane_device(p):
        return (p // 2, lax.rem(p, 2) * Z + z_at)

    def z_device(z):
        return (crop, y_at * Z + z)

    partner = (crop, (1 - y_at) * Z + z_at)

    def greet(y, z):
        device = (crop, lax.rem(y, 2) * Z + lax.rem(z, Z))
        pl.semaphore_signal(barrier, inc=1, device_id=device, device_id_type=MESH)

    greet(y_at, z_at + 8)
    greet(y_at + 1, z_at + 8)

    @pl.loop(1, 8)
    def _(s):
        greet(y_at, z_at + 8 - s)
        greet(y_at, z_at + 8 + s)
        greet(y_at + 1, z_at + 8 - s)
        greet(y_at + 1, z_at + 8 + s)

    greet(y_at + 1, z_at)

    @pl.loop(1, NP)
    def _(s):
        pl.semaphore_signal(barrier, inc=1, device_id=plane_device(lax.rem(plane_me + s, NP)), device_id_type=MESH)

    fetches = [pltpu.make_async_copy(given[k], held[k], in_sem.at[k]) for k in range(9)]
    stores = [pltpu.make_async_copy(filled[k], results[k], out_sem.at[k]) for k in range(9)]
    for k in (0, 2, 3, 5, 4, 6, 1, 7, 8):
        fetches[k].start()

    def copy_to(src, dst, k, device):
        return pltpu.make_async_remote_copy(
            src_ref=src, dst_ref=dst, send_sem=send_sem.at[k], recv_sem=recv_sem.at[k],
            device_id=device, device_id_type=MESH)

    def wait_bytes(ref, sem):
        pltpu.make_async_copy(ref, ref, sem).wait()

    sent = []

    def arrived(k, ref):
        wait_bytes(ref, recv_sem.at[k])
        sent.append((k, ref))

    def send_half(x, m):
        k = 2 * x + m
        part = pl.ds(8 * m, 8)

        def to(y, z):
            peer = lax.rem(y, 2) * Z + lax.rem(z, Z)
            copy_to(stage_ref.at[x, peer, part], recv_ref.at[x, me, part], k, (crop, peer)).start()

        to(y_at, z_at + 8)
        to(y_at + 1, z_at + 8)

        @pl.loop(1, 8)
        def _(s):
            to(y_at, z_at + 8 - s)
            to(y_at, z_at + 8 + s)
            to(y_at + 1, z_at + 8 - s)
            to(y_at + 1, z_at + 8 + s)

        to(y_at + 1, z_at)
        recv_ref[x, me, part] = stage_ref[x, me, part]

    def half_arrived(x, m):
        arrived(2 * x + m, recv_ref.at[x, pl.ds(0, D - 1), pl.ds(8 * m, 8)])

    def near_z(s):
        return lax.rem(z_at + 12 + s + s // 4, Z)

    def middle_z(s):
        return lax.rem(z_at + 5 + s + 3 * (s // 2), Z)

    def far_z(s):
        return lax.rem(z_at + 7 + s, Z)

    def gather_z(g):
        def to(y, z, k):
            copy_to(chunk_ref.at[g], gather_ref.at[g, me], k, (crop, y * Z + z)).start()

        @pl.loop(0, 3)
        def _(s):
            to(y_at, far_z(s), 10 + 4 * g)
            if g == 0:
                to(1 - y_at, far_z(s), 10 + 4 * g)

        @pl.loop(0, 4)
        def _(s):
            to(y_at, middle_z(s), 9 + 4 * g)

        @pl.loop(0, 8)
        def _(s):
            to(y_at, near_z(s), 8 + 4 * g)

        gather_ref[g, me] = chunk_ref[g]

    def forward(g):
        def to(z):
            slot = y_at * Z + z
            copy_to(gather_ref.at[g, slot], gather_ref.at[g, slot], 11 + 4 * g, partner).start()

        to(z_at)
        arrived(8 + 4 * g, gather_ref.at[g, pl.ds(0, 8)])

        @pl.loop(0, 8)
        def _(s):
            to(near_z(s))

        arrived(9 + 4 * g, gather_ref.at[g, pl.ds(0, 4)])

        @pl.loop(0, 4)
        def _(s):
            to(middle_z(s))

        if g == 1:
            arrived(10 + 4 * g, gather_ref.at[g, pl.ds(0, 3)])

            @pl.loop(0, 3)
            def _(s):
                to(far_z(s))

    def gathered(g):
        if g == 0:
            arrived(10, gather_ref.at[g, pl.ds(0, 6)])
        arrived(11 + 4 * g, gather_ref.at[g, pl.ds(0, 13 + 3 * g)])

    def reduce_y():
        copy_to(stage_ref.at[4, pl.ds((1 - y_at) * Z, Z)], pairsum_ref.at[0], 16, partner).start()

    def reduce_z():
        arrived(16, pairsum_ref.at[0])
        zstage_ref[0] = stage_ref[4, pl.ds(y_at * Z, Z)] + pairsum_ref[0]

        @pl.loop(1, Z)
        def _(s):
            z = lax.rem(z_at + s, Z)
            copy_to(zstage_ref.at[0, z], zrecv_ref.at[0, z_at], 17, z_device(z)).start()

        zrecv_ref[0, z_at] = zstage_ref[0, z_at]

    def swift_y():
        @pl.loop(0, 5)
        def _(s):
            z = lax.rem(z_at + 6 + s, Z)
            copy_to(stage_ref.at[5, y_at * Z + z], direct_ref.at[s], 28, (crop, y_at * Z + z)).start()
            other = (1 - y_at) * Z + z
            copy_to(stage_ref.at[5, other], direct_ref.at[5 + s], 28, (crop, other)).start()

        @pl.loop(0, 11)
        def _(s):
            z = lax.rem(z_at + 11 + s, Z)
            copy_to(stage_ref.at[5, (1 - y_at) * Z + z], pairsum_ref.at[1, s], 18, partner).start()

    def swift_z():
        arrived(18, pairsum_ref.at[1, pl.ds(0, 11)])

        @pl.loop(0, 11)
        def _(s):
            z = lax.rem(z_at + 11 + s, Z)
            zstage_ref[1, s] = stage_ref[5, y_at * Z + z] + pairsum_ref[1, s]

        @pl.loop(0, 5)
        def _(s):
            for at in (s, 10 - s):
                copy_to(zstage_ref.at[1, at], zrecv_ref.at[1, at], 19, z_device(lax.rem(z_at + 11 + at, Z))).start()

        zrecv_ref[1, 5] = zstage_ref[1, 5]

    def token_rows(total):
        whole = jnp.concatenate([total[i * HEADS:(i + 1) * HEADS] for i in range(R)], axis=1)
        return jnp.concatenate([whole, jnp.zeros((4, T), F32)], axis=0)

    def reduced():
        arrived(17, zrecv_ref.at[0, pl.ds(0, Z - 1)])
        return token_rows(total_of(zrecv_ref.at[0], Z))

    def swift_reduced():
        arrived(28, direct_ref)
        arrived(19, zrecv_ref.at[1, pl.ds(0, 10)])
        return token_rows(total_of(zrecv_ref.at[1], 11) + total_of(direct_ref, 10))

    def put_stage(slot, row, tile):
        stage_ref[slot, :, row, :] = tile

    def get_recv(x, row):
        return recv_ref[x, :, row, :]

    def prepare(b):
        for g in range(4):
            w = w_ref[b, g]
            if g == 0:
                w = w * scale
            hi, lo = split(w.T)
            wt_ref[b, 0, g * C:(g + 1) * C] = hi
            wt_ref[b, 1, g * C:(g + 1) * C] = lo

    def columns(b):
        rows = jnp.concatenate([gs_ref[b:b + 1], jnp.zeros((7, C), F32)], axis=0)
        return rows.T[:, 0:1]

    def bias_rows(b, x_split):
        bw = jnp.concatenate([bw_ref[b], jnp.zeros((4, C), F32)], axis=0)
        return dot3m(split(bw), x_split, NN)

    def put_chunk(slot, rows):
        for i in range(R):
            chunk_ref[slot, i * HEADS:(i + 1) * HEADS] = rows[0:HEADS, i * N:(i + 1) * N]

    def project(b, x_split):
        out = dot3((wt_ref[b, 0], wt_ref[b, 1]), x_split, NN)
        out_gate = jax.nn.sigmoid(out[3 * C:] + columns(b))
        for i in range(R):
            pt_ref[b, i, 0:3 * C] = out[0:3 * C, i * N:(i + 1) * N]
            pt_ref[b, i, 3 * C:] = out_gate[:, i * N:(i + 1) * N]

    def attend(b, lo, hi):
        for i in range(lo, hi):
            for h in range(HEADS):
                at = h * HS
                q = pt_ref[b, i, at:at + HS]
                k = pt_ref[b, i, C + at:C + at + HS]
                v = pt_ref[b, i, 2 * C + at:2 * C + at + HS]
                s = dot_tn(k, q) + bt_ref[b, h]
                e = jnp.exp(s - jnp.max(s, axis=0, keepdims=True))
                a = e * (1.0 / jnp.sum(e, axis=0, keepdims=True))
                at_ref[b, i, h] = a
                o = dot3m(split(v), split(a), NN)
                ot_ref[b, i, at:at + HS] = o
                yt_ref[b, i, at:at + HS] = o * pt_ref[b, i, 3 * C + at:3 * C + at + HS]

    def over_rows(ref, b, lo=0, hi=R):
        return jnp.concatenate([ref[b, i] for i in range(lo, hi)], axis=1)

    def update(b, lo, hi):
        ut = dot3(split(wo_ref[b].T), split(over_rows(yt_ref, b, lo, hi)), NN)
        return ut.T + os_ref[b:b + 1]

    def backward(b, du_split, lo, hi):
        dyt = dot3(split(wo_ref[b]), du_split, NT)
        for i in range(lo, hi):
            dy = dyt[:, (i - lo) * N:(i - lo + 1) * N]
            gate = pt_ref[b, i, 3 * C:]
            dot_ref[i] = dy * gate
            dpt_ref[b, i, 3 * C:] = dy * ot_ref[b, i] * (gate * (1.0 - gate))
        for i in range(lo, hi):
            for h in range(HEADS):
                at = h * HS
                q = pt_ref[b, i, at:at + HS]
                k = pt_ref[b, i, C + at:C + at + HS]
                v = pt_ref[b, i, 2 * C + at:2 * C + at + HS]
                a = at_ref[b, i, h]
                do = dot_ref[i, at:at + HS]
                row = jnp.sum(do * ot_ref[b, i, at:at + HS], axis=0, keepdims=True)
                ds = a * (dot_tn(v, do) - row)
                if i == 0:
                    db_ref[b, h] = ds
                else:
                    db_ref[b, h] += ds
                ds_split = split(ds)
                dpt_ref[b, i, at:at + HS] = dot3m(split(k), ds_split, NN)
                dpt_ref[b, i, C + at:C + at + HS] = dot3m(split(q), ds_split, NT)
                dpt_ref[b, i, 2 * C + at:2 * C + at + HS] = dot3m(split(do), split(a), NT)

    def dx_local(b, lo, hi):
        total = None
        for g in range(4):
            w = w_ref[b, g]
            if g == 0:
                w = w * scale
            d = jnp.concatenate([dpt_ref[b, i, g * C:(g + 1) * C] for i in range(lo, hi)], axis=1)
            term = dot3(split(w), split(d), NN)
            total = term if total is None else total + term
        return total

    msgs, nears, fars, lasts = (msg0_ref, msg1_ref), (near0_ref, near1_ref), (far0_ref, far1_ref), (last0_ref, last1_ref)

    def big_grads(b, x_split, du_split):
        parts = []
        for g in range(4):
            d = jnp.concatenate([dpt_ref[b, i, g * C:(g + 1) * C] for i in range(R)], axis=1)
            out = dot3(x_split, split(d), NT)
            parts.append(out * scale if g == 0 else out)
        parts.append(dot3(split(over_rows(yt_ref, b)), du_split, NN))
        whole = jnp.concatenate(parts, axis=0)
        for p in range(NP):
            big_ref[b, p] = whole[p * rows:(p + 1) * rows]

    def to_plane(src_of, dst, k):
        def to(s):
            p = lax.rem(plane_me + s, NP)
            copy_to(src_of(p), dst, k, plane_device(p)).start()

        to(NC)

        @pl.loop(1, NC)
        def _(s):
            to(NC - s)
            to(NC + s)

    def send_big(b):
        to_plane(lambda p: big_ref.at[b, p], bigr_ref.at[b, plane_me], 20 + 4 * b)
        bigr_ref[b, plane_me] = big_ref[b, plane_me]

    def total_of(ref, count):
        total = ref[0]
        for p in range(1, count):
            total = total + ref[p]
        return total

    def send_near(b):
        arrived(20 + 4 * b, bigr_ref.at[b, pl.ds(0, NP - 1)])
        msgs[b][0, 0:rows] = total_of(bigr_ref.at[b], NP)
        if b == 1:
            msgs[b][0, rows:rows + 8] = tiny_ref[b]

        @pl.loop(1, 4)
        def _(s):
            m = lax.rem(inner + s, 4)
            copy_to(msgs[b].at[0], nears[b].at[inner], 21 + 4 * b, z_device(block * 4 + m)).start()

        nears[b][inner] = msgs[b][0]

    def send_far(b):
        arrived(21 + 4 * b, nears[b].at[pl.ds(0, 3)])
        msgs[b][1] = total_of(nears[b], 4)

        @pl.loop(1, 4)
        def _(s):
            m = lax.rem(block + s, 4)
            copy_to(msgs[b].at[1], fars[b].at[block], 22 + 4 * b, z_device(m * 4 + inner)).start()

        fars[b][block] = msgs[b][1]

    def send_z(b):
        arrived(20 + 4 * b, bigr_ref.at[b, pl.ds(0, NP - 1)])
        msgs[b][0] = total_of(bigr_ref.at[b], NP)

        def to(s):
            copy_to(msgs[b].at[0], column_ref.at[z_at], 21 + 4 * b, z_device(lax.rem(z_at + s, Z))).start()

        to(8)

        @pl.loop(1, 8)
        def _(s):
            to(8 - s)
            to(8 + s)

        column_ref[z_at] = msgs[b][0]

    def send_last(b):
        if b == 0:
            arrived(21, column_ref.at[pl.ds(0, Z - 1)])
            msgs[b][2] = total_of(column_ref, Z) * out_scale
        else:
            arrived(22 + 4 * b, fars[b].at[pl.ds(0, 3)])
            msgs[b][2] = total_of(fars[b], 4) * out_scale
        to_plane(lambda p: msgs[b].at[2], lasts[b].at[plane_me], 23 + 4 * b)
        lasts[b][plane_me] = msgs[b][2]

    def finish_big(b):
        arrived(23 + 4 * b, lasts[b].at[pl.ds(0, NP - 1)])
        for p in range(NP):
            first = p * rows
            while first < (p + 1) * rows:
                g, at = first // C, first % C
                count = min((p + 1) * rows - first, C - at)
                piece = lasts[b][p, first - p * rows:first - p * rows + count]
                if g < 4:
                    gproj_ref[b, g, at:at + count] = piece
                else:
                    gout_ref[b, at:at + count] = piece
                first += count

    def put_tiny(b, tiny):
        ggain_ref[b:b + 1] = tiny[0:1]
        gshift_ref[b:b + 1] = tiny[1:2]
        gbias_ref[b] = tiny[2:2 + HEADS]
        ggate_ref[b:b + 1] = tiny[6:7]
        gos_ref[b:b + 1] = tiny[7:8]

    def send_tiny_z():
        @pl.loop(1, Z)
        def _(s):
            copy_to(tiny_ref.at[0], tinyz_ref.at[z_at], 29, z_device(lax.rem(z_at + s, Z))).start()

        tinyz_ref[z_at] = tiny_ref[0]

    def send_tiny_plane():
        arrived(29, tinyz_ref.at[pl.ds(0, Z - 1)])
        tiny_ref[2] = total_of(tinyz_ref, Z)
        to_plane(lambda p: tiny_ref.at[2], tinyp_ref.at[plane_me], 30)
        tinyp_ref[plane_me] = tiny_ref[2]

    def finish_tiny():
        arrived(30, tinyp_ref.at[pl.ds(0, NP - 1)])
        put_tiny(0, total_of(tinyp_ref, NP) * out_scale)

    def gate_grad(b):
        total = None
        for i in range(R):
            d = dpt_ref[b, i, 3 * C:]
            total = d if total is None else total + d
        return jnp.sum(total.T, axis=0, keepdims=True)

    def bias_part(b, dbr, x_split):
        bw = jnp.concatenate([bw_ref[b], jnp.zeros((4, C), F32)], axis=0)
        d_split = split(dbr)
        dxt = dot3(split(bw.T), d_split, NN)
        dbw = dot3m(d_split, x_split, NT)
        return dxt, dbw[0:HEADS]

    def col_sum(x):
        return jnp.sum(x, axis=0, keepdims=True)

    fetches[0].wait()
    for i in range(R):
        for j in range(R):
            at = (i * R + j) * D
            z_ref[0, at:at + D] = pair_ref[pl.ds(i * N + j, D, stride=R)]
    fetches[2].wait()
    fetches[3].wait()
    fetches[5].wait()
    n0, r0 = normalise(z_ref[0])
    n_ref[0] = n0
    r_ref[0] = r0
    x0_split = split((n0 * gain_ref[0:1] + shift_ref[0:1]).T)
    xt_ref[0, 0] = x0_split[0]
    xt_ref[0, 1] = x0_split[1]
    put_chunk(0, bias_rows(0, x0_split))
    fetches[4].wait()
    fetches[6].wait()
    prepare(0)
    pl.semaphore_wait(barrier, D - 1 + NP - 1)
    gather_z(0)
    fetches[1].wait()
    for i in range(R):
        for j in range(R):
            at = (i * R + j) * D
            tile = grad_ref[pl.ds(i * N + j, D, stride=R)]
            up_ref[at:at + D] = tile
            put_stage(0, j * R + i, tile)
    project(0, x0_split)
    forward(0)
    send_half(0, 0)
    prepare(1)
    fetches[7].wait()
    fetches[8].wait()
    gathered(0)
    for h in range(HEADS):
        bt_ref[0, h] = jnp.concatenate([gather_ref[0, :, i * HEADS + h, :] for i in range(R)], axis=0).T

    for m in range(2):
        attend(0, 2 * m, 2 * m + 2)
        part = slice(2 * m * N, (2 * m + 2) * N)
        z_ref[1, part] = z_ref[0, part] + update(0, 2 * m, 2 * m + 2)
        for row in range(8 * m, 8 * m + 8):
            put_stage(1, row, z_ref[1, row * D:(row + 1) * D])
        if m == 0:
            send_half(1, 0)
    nm, rm = normalise(z_ref[1])
    nm_ref[...] = nm
    rm_ref[...] = rm
    xm_split = split((nm * gain_ref[1:2] + shift_ref[1:2]).T)
    xt_ref[2, 0] = xm_split[0]
    xt_ref[2, 1] = xm_split[1]
    put_chunk(1, bias_rows(1, xm_split))
    gather_z(1)
    send_half(1, 1)
    forward(1)

    half_arrived(1, 0)
    send_half(0, 1)
    half_arrived(1, 1)
    n1, r1 = normalise(
        jnp.concatenate([get_recv(1, i * R + j) for j in range(R) for i in range(R)], axis=0))
    n_ref[1] = n1
    r_ref[1] = r1
    x1_split = split((n1 * gain_ref[1:2] + shift_ref[1:2]).T)
    xt_ref[1, 0] = x1_split[0]
    xt_ref[1, 1] = x1_split[1]
    project(1, x1_split)
    gathered(1)
    for h in range(HEADS):
        bt_ref[1, h] = jnp.concatenate([gather_ref[1, :, i * HEADS + h, :] for i in range(R)], axis=0)

    def stage_back(slot, m, value):
        for row in range(8):
            put_stage(slot, 8 * m + row, value[row * D:(row + 1) * D])

    for m in range(2):
        attend(1, 2 * m, 2 * m + 2)
        stage_back(2, m, update(1, 2 * m, 2 * m + 2))

    du1_halves = []
    for m in range(2):
        part = slice(2 * m * N, (2 * m + 2) * N)
        half_arrived(0, m)
        du1_halves.append(jnp.concatenate([get_recv(0, 8 * m + row) for row in range(8)], axis=0))
        backward(1, split(du1_halves[m]), 2 * m, 2 * m + 2)
        if m == 1:
            for h in range(HEADS):
                for i in range(R):
                    put_stage(4, i * HEADS + h, db_ref[1, h, i * D:(i + 1) * D])
            reduce_y()
        dx = dx_local(1, 2 * m, 2 * m + 2).T
        dx_ref[part] = dx
        stage_back(3, m, normalise_back(dx * gain_ref[1:2], n_ref[1, part], r_ref[1, part]))
        send_half(3, m)
    reduce_z()
    du1 = jnp.concatenate(du1_halves, axis=0)
    big_grads(1, (xt_ref[1, 0], xt_ref[1, 1]), split(du1))
    send_big(1)
    tiny_ref[1, 0:1] = col_sum(dx_ref[...] * n_ref[1])
    tiny_ref[1, 1:2] = col_sum(dx_ref[...])
    tiny_ref[1, 6:7] = gate_grad(1)
    tiny_ref[1, 7:8] = col_sum(du1)
    dxm_t, dbw1 = bias_part(1, reduced(), (xt_ref[2, 0], xt_ref[2, 1]))
    dxm = dxm_t.T
    tiny_ref[1, 0:1] += col_sum(dxm * nm_ref[...])
    tiny_ref[1, 1:2] += col_sum(dxm)
    tiny_ref[1, 2:2 + HEADS] = dbw1
    mg_ref[...] = up_ref[...] + normalise_back(dxm * gain_ref[1:2], nm_ref[...], rm_ref[...])
    send_near(1)
    half_arrived(3, 0)
    half_arrived(3, 1)
    send_half(2, 0)
    for i in range(R):
        for j in range(R):
            at = (i * R + j) * D
            mg_ref[at:at + D] += get_recv(3, j * R + i)

    du0_split = split(mg_ref[...])
    backward(0, du0_split, 0, R)
    for h in range(HEADS):
        turned = db_ref[0, h].T
        for i in range(R):
            put_stage(5, i * HEADS + h, turned[i * D:(i + 1) * D])
    swift_y()
    send_far(1)
    big_grads(0, (xt_ref[0, 0], xt_ref[0, 1]), du0_split)
    swift_z()
    send_big(0)
    tiny_ref[0, 6:7] = gate_grad(0)
    tiny_ref[0, 7:8] = col_sum(mg_ref[...])
    dxt_ref[...] = dx_local(0, 0, R)
    send_z(0)
    dx0_t, dbw0 = bias_part(0, swift_reduced(), (xt_ref[0, 0], xt_ref[0, 1]))
    dx_ref[...] = (dxt_ref[...] + dx0_t).T
    tiny_ref[0, 0:1] = col_sum(dx_ref[...] * n_ref[0])
    tiny_ref[0, 1:2] = col_sum(dx_ref[...])
    tiny_ref[0, 2:2 + HEADS] = dbw0
    send_tiny_z()
    send_half(2, 1)
    dz0 = normalise_back(dx_ref[...] * gain_ref[0:1], n_ref[0], r_ref[0])
    for i in range(R):
        for j in range(R):
            at = (i * R + j) * D
            igrad_ref[pl.ds(i * N + j, D, stride=R)] = mg_ref[at:at + D] + dz0[at:at + D]
    stores[1].start()
    send_tiny_plane()
    send_last(0)
    send_last(1)
    for j in range(R):
        if j % 2 == 0:
            half_arrived(2, j // 2)
        for i in range(R):
            at = (i * R + j) * D
            new_ref[pl.ds(i * N + j, D, stride=R)] = z_ref[1, at:at + D] + get_recv(2, j * R + i)
    stores[0].start()
    finish_big(1)
    tiny1 = last1_ref[0, rows:rows + 8]
    for p in range(1, NP):
        tiny1 = tiny1 + last1_ref[p, rows:rows + 8]
    put_tiny(1, tiny1)
    finish_tiny()
    finish_big(0)

    for k in range(2, 9):
        stores[k].start()

    for k, ref in sent:
        wait_bytes(ref, send_sem.at[k])
    for store in stores:
        store.wait()


def copies(*refs):
    ins, outs, held, sems = refs[:9], refs[9:18], refs[18:27], refs[27]
    fetches = [pltpu.make_async_copy(ins[k], held[k], sems.at[0, k]) for k in range(9)]
    stores = [pltpu.make_async_copy(held[k], outs[k], sems.at[1, k]) for k in range(9)]
    for fetch in fetches:
        fetch.start()
    for fetch, store in zip(fetches, stores):
        fetch.wait()
        store.start()
    for store in stores:
        store.wait()


def body(D, NC, pair, pair_grad, gain, shift, w, bw, gs, wo, os):
    R, N, C = pair.shape[1:]
    T = R * N
    NP = 2 * NC
    rows = 5 * C // NP
    anywhere = pl.BlockSpec(memory_space=pl.ANY)
    out = lambda *shape: jax.ShapeDtypeStruct(shape, F32)
    args = (pair.reshape(T, C), pair_grad.reshape(T, C), gain, shift, w, bw, gs, wo, os)
    shapes_in = [out(*a.shape) for a in args]
    shapes_out = [out(T, C), out(T, C), out(2, C), out(2, C), out(2, 4, C, C), out(2, HEADS, C), out(2, C),
                  out(2, C, C), out(2, C)]
    results = pl.pallas_call(
        functools.partial(kernel, D, NC),
        out_shape=shapes_out,
        in_specs=[anywhere] * 9,
        out_specs=[anywhere] * 9,
        scratch_shapes=[pltpu.VMEM(s.shape, F32) for s in shapes_in + shapes_out] + [
            pltpu.SemaphoreType.DMA((9,)),
            pltpu.SemaphoreType.DMA((9,)),
            pltpu.VMEM((2, T, C), F32),
            pltpu.VMEM((2, T, C), F32),
            pltpu.VMEM((2, T, 1), F32),
            pltpu.VMEM((T, C), F32),
            pltpu.VMEM((T, 1), F32),
            pltpu.VMEM((T, C), F32),
            pltpu.VMEM((T, C), F32),
            pltpu.VMEM((T, C), F32),
            pltpu.VMEM((C, T), F32),
            pltpu.VMEM((2, 2, 4 * C, C), BF16),
            pltpu.VMEM((3, 2, C, T), BF16),
            pltpu.VMEM((2, R, 4 * C, N), F32),
            pltpu.VMEM((2, R, HEADS, N, N), F32),
            pltpu.VMEM((2, R, C, N), F32),
            pltpu.VMEM((2, R, C, N), F32),
            pltpu.VMEM((R, C, N), F32),
            pltpu.VMEM((2, R, 4 * C, N), F32),
            pltpu.VMEM((2, HEADS, N, N), F32),
            pltpu.VMEM((2, HEADS, N, N), F32),
            pltpu.VMEM((6, D, R * R, C), F32),
            pltpu.VMEM((2, R * R, N), F32),
            pltpu.VMEM((4, D, R * R, C), F32),
            pltpu.VMEM((2, D, R * R, C), F32),
            pltpu.VMEM((2, Z, R * R, C), F32),
            pltpu.VMEM((2, Z, R * R, C), F32),
            pltpu.VMEM((2, Z, R * R, C), F32),
            pltpu.VMEM((10, R * R, C), F32),
            pltpu.VMEM((2, NP, rows, C), F32),
            pltpu.VMEM((2, NP, rows, C), F32),
            pltpu.VMEM((3, rows, C), F32),
            pltpu.VMEM((3, rows + 8, C), F32),
            pltpu.VMEM((4, rows, C), F32),
            pltpu.VMEM((4, rows + 8, C), F32),
            pltpu.VMEM((4, rows, C), F32),
            pltpu.VMEM((4, rows + 8, C), F32),
            pltpu.VMEM((NP, rows, C), F32),
            pltpu.VMEM((NP, rows + 8, C), F32),
            pltpu.VMEM((3, 8, C), F32),
            pltpu.VMEM((Z, 8, C), F32),
            pltpu.VMEM((NP, 8, C), F32),
            pltpu.VMEM((Z, rows, C), F32),
            pltpu.SemaphoreType.DMA((31,)),
            pltpu.SemaphoreType.DMA((31,)),
        ],
        compiler_params=pltpu.CompilerParams(
            collective_id=0, has_side_effects=True, vmem_limit_bytes=56 * 1024 * 1024),
    )(*args)
    results = pl.pallas_call(
        copies,
        out_shape=shapes_out,
        in_specs=[anywhere] * 9,
        out_specs=[anywhere] * 9,
        scratch_shapes=[pltpu.VMEM(s.shape, F32) for s in shapes_out] + [pltpu.SemaphoreType.DMA((2, 9))],
        compiler_params=pltpu.CompilerParams(vmem_limit_bytes=56 * 1024 * 1024),
    )(*results)
    return (results[0].reshape(pair.shape), results[1].reshape(pair.shape)) + tuple(results[2:])


def solution(mesh):
    rows = P("crop", "dap", None, None)
    return jax.shard_map(
        functools.partial(body, mesh.shape["dap"], mesh.shape["crop"]),
        mesh=mesh,
        in_specs=(rows, rows) + (P(),) * 7,
        out_specs=(rows, rows) + (P(),) * 7,
        check_vma=False,
    )
```
